512 devices in a mesh: member: 16 (over z_hi, y), gx: 8 (over z_lo, core), gy: 4 (over x).
Axes of the slice: x: 4, y: 4, z: 16 (z_hi: 4, z_lo: 4; z = z_hi * 4 + z_lo), core: 2. Of those that a mesh axis runs over, the one named last changes fastest.
Arguments:
- density: float32 [16, 64, 256, 512], P('member', None, 'gx', 'gy'), may hold values from 0.1 to 2
- turn_rate: bfloat16 [16, 64, 256, 512], P('member', None, 'gx', 'gy'), may hold values from -0.19921875 to 0.19921875
- value_init: float32 [64, 256, 512], P(None, 'gx', 'gy'), may hold values from -33 to 3
- labels: int32 [256, 512], P('gx', 'gy'), may hold values from 0 to 7
- counts: int32 [16], replicated, may hold values from 1 to 16
- kernel: float32 [64, 64], replicated, may hold values from -4 to 4
Outputs:
- moved: float32 [16, 64, 256, 512], P('member', None, 'gx', 'gy')
- values: float32 [64, 256, 512], P(None, 'gx', 'gy')
The draws below stay inside these ranges and needn't reach their ends.
All inputs are finite; a program needn't handle non-finite values.
Results may differ from the reference program's by a relative error of at most 0.0003.
Values may be sent and summed in bfloat16 or wider, within the bound.
A program may use at most 64 MiB of HBM per device.

```python
import math
import jax
import jax.numpy as jnp
from jax import lax

H = 64
MEMBERS = 16
NX = 256
NY = 512


def draw_value_init(key, part):
    key = jax.random.fold_in(key, 5)
    first = jax.random.fold_in(key, 0)
    base = jnp.clip(jax.random.normal(first, (H, NX, NY), jnp.float32), -3.0, 3.0)
    return base


def touch_ends(entries, key, smallest, top_value):
    shape = entries.shape
    index_at = [jax.random.randint(jax.random.fold_in(key, axis), (), 0, shape[axis]) for axis in range(len(shape))]
    entries = entries.at[tuple(index_at)].set(smallest)
    longest = shape.index(max(shape))
    index_at[longest] = (index_at[longest] + 1) % shape[longest]
    return entries.at[tuple(index_at)].set(top_value)


def level_of(key, extent, cuts, smallest, largest):
    loudness, own = 1.0, jax.random.fold_in(key, 6)
    for dim, parts in cuts:
        draws = jnp.exp(jax.random.uniform(jax.random.fold_in(own, dim), (parts,), jnp.float32, smallest / len(cuts), largest / len(cuts)))
        loudness = loudness * jnp.repeat(draws, extent[dim] // parts).reshape([-1 if axis == dim else 1 for axis in range(len(extent))])
    return loudness


def centred(key, shape, width, reach, kind=jnp.bfloat16):
    drawn = jax.random.normal(key, shape, jnp.float32) * width
    return jnp.minimum(jnp.maximum(drawn, -reach), reach).astype(kind)


def setup_inputs(seed: int = 0) -> dict:
    arg_keys = jax.random.split(jax.random.key(seed), 7)
    return {
        "density": jnp.clip(jnp.exp(math.log(2.0) - 2.9957323 * jax.random.uniform(arg_keys[0], (MEMBERS, H, NX, NY), jnp.float32) ** level_of(arg_keys[0], (MEMBERS, H, NX, NY), ((0, 16), (2, 8), (3, 4)), -0.2, 0.2)), 0.1, 2.0),
        "turn_rate": jnp.clip(jax.random.uniform(arg_keys[1], (MEMBERS, H, NX, NY), jnp.float32, -0.19921875, 0.19921875) * level_of(arg_keys[1], (MEMBERS, H, NX, NY), ((0, 16), (2, 8), (3, 4)), -0.4, 0.0), -0.19921875, 0.19921875).astype(jnp.bfloat16),
        "value_init": draw_value_init(jax.random.fold_in(arg_keys[6], 71), 0),
        "labels": touch_ends(jax.random.randint(arg_keys[3], (NX, NY), 0, 8), jax.random.fold_in(arg_keys[3], 1), 0, 7).astype(jnp.int32),
        "counts": touch_ends(jax.random.randint(arg_keys[4], (MEMBERS,), 1, 17), jax.random.fold_in(arg_keys[4], 1), 1, 16).astype(jnp.int32),
        "kernel": centred(arg_keys[5], (H, H), 1.0, 4.0, jnp.float32),
    }


speed_scale = 0.55
temper = 0.1
time_step = 0.5
turn_cost = 0.5


def heading_tables(count):
    angles = jnp.arange(count).astype(jnp.float32) * (2.0 * jnp.pi / count)
    along_x = (speed_scale * jnp.cos(angles)).reshape(count, 1, 1)
    along_y = (speed_scale * jnp.sin(angles)).reshape(count, 1, 1)
    spread = angles[:, None] - angles[None, :]
    coupling = jnp.exp(-turn_cost * (1.0 - jnp.cos(spread)) / temper)
    return (jnp.maximum(along_x, 0.0), jnp.maximum(-along_x, 0.0),
            jnp.maximum(along_y, 0.0), jnp.maximum(-along_y, 0.0), coupling)


def edge_weights(opened):
    center = opened[1:-1, 1:-1]
    return (center * opened[2:, 1:-1], center * opened[:-2, 1:-1],
            center * opened[1:-1, 2:], center * opened[1:-1, :-2])


def transport(masses, opened, turning, absorb):
    east_rate, west_rate, north_rate, south_rate, coupling = heading_tables(masses.shape[0])
    to_east, to_west, to_north, to_south = edge_weights(opened)
    center = masses[:, 1:-1, 1:-1]
    leaving = center * (east_rate * to_east + west_rate * to_west + north_rate * to_north + south_rate * to_south)
    arriving = (east_rate * to_west * masses[:, :-2, 1:-1] + west_rate * to_east * masses[:, 2:, 1:-1]
                + north_rate * to_south * masses[:, 1:-1, :-2] + south_rate * to_north * masses[:, 1:-1, 2:])
    turn_up = jnp.maximum(turning, 0.0)
    turn_down = jnp.maximum(-turning, 0.0)
    rotated = (jnp.roll(turn_up * center, 1, axis=0) + jnp.roll(turn_down * center, -1, axis=0)
               - (turn_up + turn_down) * center)
    return (center - leaving + arriving + rotated) * (1.0 - absorb)


def best_reply(widened, opened, running, absorb):
    east_rate, west_rate, north_rate, south_rate, coupling = heading_tables(widened.shape[0])
    to_east, to_west, to_north, to_south = edge_weights(opened)
    center = widened[:, 1:-1, 1:-1]
    moves = (center + east_rate * to_east * (widened[:, 2:, 1:-1] - center)
             + west_rate * to_west * (widened[:, :-2, 1:-1] - center)
             + north_rate * to_north * (widened[:, 1:-1, 2:] - center)
             + south_rate * to_south * (widened[:, 1:-1, :-2] - center))
    lowest = jnp.min(moves, axis=0)
    scaled = jnp.exp((lowest - moves) / temper)
    count = moves.shape[0]
    summed = jnp.dot(coupling, scaled.reshape(count, -1), precision=lax.Precision.HIGHEST).reshape(moves.shape)
    return (time_step * running + lowest - temper * jnp.log(summed)) * (1.0 - absorb)


def congestion(kernel, mixed):
    count = mixed.shape[0]
    return 1.0 + jnp.dot(kernel, mixed.reshape(count, -1), precision=lax.Precision.HIGHEST).reshape(mixed.shape)


def reference(density, turn_rate, value_init, labels, counts, kernel):
    opened = jnp.pad((labels != 1).astype(jnp.float32), 1)
    absorb = (labels == 2).astype(jnp.float32)

    def advance(paired):
        masses, turning = paired
        turning = turning.astype(jnp.float32)
        for repeat in range(2):
            masses = transport(jnp.pad(masses, ((0, 0), (1, 1), (1, 1))), opened, turning, absorb)
        return masses

    moved = lax.map(advance, (density, turn_rate))
    weights = counts.astype(jnp.float32)
    shares = weights / jnp.sum(weights)
    mixed = jnp.sum(shares[:, None, None, None] * moved, axis=0)
    running = congestion(kernel, mixed)
    values = value_init
    for repeat in range(2):
        values = best_reply(jnp.pad(values, ((0, 0), (1, 1), (1, 1))), opened, running, absorb)
    return moved, values
```

```python
import jax
import jax.numpy as jnp
import numpy as np
from jax import lax
from jax.experimental import pallas as pl
from jax.experimental.pallas import tpu as pltpu
from jax.sharding import PartitionSpec as P

MESH = pl.DeviceIdType.MESH
F32 = jnp.float32
BF16 = jnp.bfloat16
I16 = jnp.int16
I32 = jnp.int32

H, X, Y = 64, 32, 128
SPEED = 0.55
BOUND = 9.5

ROW_UP, ROW_DOWN, COL_UP, COL_DOWN, VAL_UP, VAL_DOWN = range(6)
STEP_ROW, STEP_COL, OVER_Y, OVER_Z, REPLY, GATHER = 6, 10, 14, 26, 34, 38
COPIES = 44


def tables():
    angles = np.arange(H, dtype=np.float32) * np.float32(2.0 * np.pi / H)
    along_x = np.abs(SPEED * np.cos(angles)).astype(np.float32)
    along_y = np.abs(SPEED * np.sin(angles)).astype(np.float32)
    spread = angles[:, None] - angles[None, :]
    coupling = np.exp(-5.0 * (1.0 - np.cos(spread.astype(np.float64)))).astype(np.float32)
    wide = lambda v: np.ascontiguousarray(np.broadcast_to(v[:, None], (H, Y)))
    return wide(along_x), wide(along_y), coupling


def encode(x):
    root = jnp.sqrt(jnp.maximum(x, 0.0)) * 65535.0 + 0.5
    return (root.astype(I32) - 32768).astype(I16)


def decode(code):
    root = code.astype(I32).astype(F32) + 32768.0
    return root * root * (BOUND / (65535.0 * 65535.0))


def split_left(m):
    high = m.astype(BF16)
    low = (m - high.astype(F32)).astype(BF16)
    return high, low


def widen(m):
    high, low = split_left(m)
    return jnp.concatenate([high, low, high, low], axis=0)


def kernel(
    counts, density, turn_hbm, value_hbm, labels_hbm, ax_hbm, ay_hbm, coupling_hbm, kernel_hbm,
    moved, values,
    r0, turn, val, labels, axt, ayt, coupling, kern,
    sx_m, sx_p, sy_m, sy_p, sv_m, sv_p, hx_m, hx_p, hy_m, hy_p, hv_m, hv_p,
    r1, r2, s2x, s2y, h2x, h2y, weights, keep,
    ysend, yrecv, zsend, zrecv, total, base,
    up_row, down_row, cs, kf, cf,
    sr_m, sr_p, sc_m, sc_p, hr_m, hr_p, hc_m, hc_p,
    gsend, grecv, out,
    load_sem, out_sem, ss, rs,
):
    member = lax.axis_index("member")
    gx = lax.axis_index("gx")
    gy = lax.axis_index("gy")
    zh, y = member // 4, member % 4
    odd = gx % 2
    q = jnp.where(odd == 1, 3 - y, y)
    turn_sign = jnp.where(odd == 1, 3, 1)

    def at(z, yy):
        return {"member": z * 4 + yy}

    pair = (jnp.where(zh % 2 == 0, zh + 1, zh - 1), 3 - zh)

    barrier = pltpu.get_barrier_semaphore()
    greeted = [at(zh, (y + d) % 4) for d in (1, 2, 3)] + [at(p, y) for p in pair]
    greeted += [{"gx": (gx + d) % 8} for d in (1, 7)] + [{"gy": (gy + d) % 4} for d in (1, 3)]
    for target in greeted:
        pl.semaphore_signal(barrier, inc=1, device_id=target, device_id_type=MESH)

    loads = [
        pltpu.make_async_copy(src, dst, load_sem.at[i])
        for i, (src, dst) in enumerate((
            (density, r0), (labels_hbm, labels), (value_hbm, val), (turn_hbm, turn), (ax_hbm, axt), (ay_hbm, ayt),
            (coupling_hbm, coupling), (kernel_hbm, kern),
        ))
    ]
    for c in loads:
        c.start()

    def copy(i, src, dst, target):
        return pltpu.make_async_remote_copy(
            src_ref=src, dst_ref=dst, send_sem=ss.at[i], recv_sem=rs.at[i], device_id=target, device_id_type=MESH
        )

    has_m, has_p = gx > 0, gx < 7
    west, east = gy > 0, gy < 3
    to_m, to_p = {"gx": (gx + 7) % 8}, {"gx": (gx + 1) % 8}
    to_w, to_e = {"gy": (gy + 3) % 4}, {"gy": (gy + 1) % 4}
    lane = lax.broadcasted_iota(I32, (X, Y), 1)
    row = lax.broadcasted_iota(I32, (X, Y), 0)
    lane_h = lax.broadcasted_iota(I32, (32, Y), 1)

    def shift_x(r, halo, k):
        if k in (0, 3):
            return jnp.where(row == 0, halo, pltpu.roll(r, 1, 0))
        return jnp.where(row == X - 1, halo, pltpu.roll(r, X - 1, 0))

    def shift_y(r, halo, position, k):
        if k in (0, 1):
            moved_halo = pltpu.roll(halo, lax.rem(Y - position, Y), 1)
            return jnp.where(lane == 0, moved_halo, pltpu.roll(r, 1, 1))
        moved_halo = pltpu.roll(halo, Y - 1 - position, 1)
        return jnp.where(lane == Y - 1, moved_halo, pltpu.roll(r, Y - 1, 1))

    def pack_column(acc, r, position, k):
        shift = position + 1 if k in (0, 1) else position
        return jnp.where(lane == position, pltpu.roll(r, shift, 1), acc)

    loads[0].wait()
    loads[1].wait()
    opened = jnp.where(labels[...] != 1, 1.0, 0.0).astype(F32)
    keep[...] = jnp.where(labels[...] == 2, 0.0, 1.0).astype(F32)
    zero_plane = jnp.zeros((X, Y), F32)

    def rows_of(ref, h0, n, x):
        return ref.reshape(H * X, Y)[pl.ds(h0 * X + x, n, stride=X), :]

    sx_p[0:16, :] = rows_of(r0, 0, 16, X - 1)
    sx_p[16:32, :] = rows_of(r0, 48, 16, X - 1)
    sx_p[32:40, :] = jnp.broadcast_to(opened[X - 1:X, :], (8, Y))
    sx_m[0:32, :] = rows_of(r0, 16, 32, 0)
    sx_m[32:40, :] = jnp.broadcast_to(opened[0:1, :], (8, Y))

    for k0, dst, shift in ((0, sy_p, 65), (2, sy_m, 64)):
        def pack(j, acc, k0=k0):
            return pack_column(acc, r0[k0 * 16 + j], j, k0)
        acc = lax.fori_loop(0, 32, pack, zero_plane, unroll=4)
        dst[0:32, :] = jnp.where(lane == 64, pltpu.roll(opened, shift, 1), acc)

    def value_row(i):
        return val.reshape(H * X, Y)[pl.ds(q * 8 + i, H, stride=X), :]

    def pack_values(rows, headings, side):
        acc = jnp.zeros((32, Y), F32)
        for i in range(8):
            part = rows[i][headings:headings + 32, :]
            shift = i + 1 if side else i
            acc = jnp.where(lane_h == i, pltpu.roll(part, shift, 1) if shift else part, acc)
        return acc

    loads[2].wait()
    own = [value_row(i) for i in range(8)]
    sy_p[32:64, :] = pack_values(own, 32, True)
    sy_m[32:64, :] = pack_values(own, 0, False)
    sv_p[...] = own[7][16:48, :]
    sv_m[0:16, :] = own[0][0:16, :]
    sv_m[16:32, :] = own[0][48:64, :]

    @pl.when(gx == 0)
    def _():
        hx_m[...] = jnp.zeros((40, Y), F32)
        hv_m[...] = jnp.zeros((32, Y), F32)
        h2x[0] = jnp.zeros((16, Y), F32)
        h2x[3] = jnp.zeros((16, Y), F32)

    @pl.when(gx == 7)
    def _():
        hx_p[...] = jnp.zeros((40, Y), F32)
        hv_p[...] = jnp.zeros((32, Y), F32)
        h2x[1] = jnp.zeros((16, Y), F32)
        h2x[2] = jnp.zeros((16, Y), F32)

    @pl.when(gy == 0)
    def _():
        hy_m[...] = jnp.zeros((64, Y), F32)
        hc_m[...] = jnp.zeros((32, Y), F32)
        h2y[0] = zero_plane
        h2y[1] = zero_plane

    @pl.when(gy == 3)
    def _():
        hy_p[...] = jnp.zeros((64, Y), F32)
        hc_p[...] = jnp.zeros((32, Y), F32)
        h2y[2] = zero_plane
        h2y[3] = zero_plane

    low, high = q == 0, q == 3
    near_up = {"member": zh * 4 + jnp.where(low, y, (y + 4 - turn_sign) % 4), "gx": jnp.where(low, (gx + 7) % 8, gx)}
    near_down = {"member": zh * 4 + jnp.where(high, y, (y + turn_sign) % 4), "gx": jnp.where(high, (gx + 1) % 8, gx)}
    has_up, has_down = jnp.logical_or(q > 0, has_m), jnp.logical_or(q < 3, has_p)

    @pl.when(jnp.logical_not(has_up))
    def _():
        hr_m[...] = jnp.zeros((32, Y), F32)

    @pl.when(jnp.logical_not(has_down))
    def _():
        hr_p[...] = jnp.zeros((32, Y), F32)

    first = (
        (copy(ROW_DOWN, sx_p, hx_m, to_p), has_p, has_m),
        (copy(ROW_UP, sx_m, hx_p, to_m), has_m, has_p),
        (copy(COL_DOWN, sy_p, hy_m, to_e), east, west),
        (copy(COL_UP, sy_m, hy_p, to_w), west, east),
        (copy(VAL_DOWN, sv_p, hv_m, to_p), jnp.logical_and(high, has_p), jnp.logical_and(low, has_m)),
        (copy(VAL_UP, sv_m, hv_p, to_m), jnp.logical_and(low, has_m), jnp.logical_and(high, has_p)),
    )

    def start(c, condition):
        @pl.when(condition)
        def _():
            c.start()

    def wait_recv(c, condition):
        @pl.when(condition)
        def _():
            c.wait_recv()

    def wait_send(c, condition):
        @pl.when(condition)
        def _():
            c.wait_send()

    pl.semaphore_wait(barrier, len(greeted))
    for c, sends, _ in first:
        start(c, sends)
    for c in loads[3:]:
        c.wait()
    kf[:, 0:64] = kern[...]
    kf[:, 64:128] = kern[...]
    for c, _, receives in first[:4]:
        wait_recv(c, receives)

    open_p = jnp.where(row == X - 1, hx_p[32:33, :], pltpu.roll(opened, X - 1, 0))
    open_m = jnp.where(row == 0, hx_m[32:33, :], pltpu.roll(opened, 1, 0))
    open_e = jnp.where(lane == Y - 1, pltpu.roll(hy_p[0:32, :], 63, 1), pltpu.roll(opened, Y - 1, 1))
    open_w = jnp.where(lane == 0, pltpu.roll(hy_m[0:32, :], 64, 1), pltpu.roll(opened, 1, 1))
    weights[0] = opened * open_p
    weights[1] = opened * open_m
    weights[2] = opened * open_e
    weights[3] = opened * open_w

    def transport(k, src, dst, halo_x, x_at, halo_y, y_at, pack):
        out_x, in_x = (0, 1) if k in (0, 3) else (1, 0)
        out_y, in_y = (2, 3) if k in (0, 1) else (3, 2)
        wox, wix, woy, wiy = weights[out_x], weights[in_x], weights[out_y], weights[in_y]
        kept = keep[...]
        columns = halo_y[0:32, :] if y_at is not None else halo_y[k]
        h0 = 16 * k
        y_from = 0 if y_at is None else y_at

        def turns(h):
            r = src[h]
            t = turn[h].astype(F32)
            up = jnp.maximum(t, 0.0) * r
            return r, up, up - t * r

        def start_of(j):
            h = h0 + j
            r, up, down = turns(h)
            ax = axt[pl.ds(h, 1), :]
            ay = ayt[pl.ds(h, 1), :]
            hx = halo_x[pl.ds(x_at + j, 1), :] if x_at is not None else halo_x[k, pl.ds(j, 1), :]
            xn = shift_x(r, hx, k)
            yn = shift_y(r, columns, y_from + j, k)
            s = r - up - down + ax * (wix * xn - wox * r) + ay * (wiy * yn - woy * r)
            return s, up, down

        _, up_before, _ = turns((h0 + 63) % 64)
        s, up, _ = start_of(0)
        carry = (s + up_before, up, zero_plane)

        def finish(j, partial, down, acc):
            new = (partial + down) * kept
            dst[h0 + j] = new
            return pack_column(acc, new, j, k) if pack else acc

        def body(j, carry):
            partial, up_last, acc = carry
            s, up, down = start_of(j)
            acc = finish(j - 1, partial, down, acc)
            return s + up_last, up, acc

        partial, _, acc = lax.fori_loop(1, 16, body, carry, unroll=3)
        _, _, down = turns((h0 + 16) % 64)
        return finish(15, partial, down, acc)

    second = []
    for k in range(4):
        halo_x, x_at = ((hx_m, 0), (hx_p, 0), (hx_p, 16), (hx_m, 16))[k]
        halo_y, y_at = ((hy_m, 0), (hy_m, 16), (hy_p, 0), (hy_p, 16))[k]
        acc = transport(k, r0, r1, halo_x, x_at, halo_y, y_at, True)
        s2y[k] = acc
        s2x[k] = rows_of(r1, 16 * k, 16, X - 1 if k in (0, 3) else 0)
        if k in (0, 3):
            rows = (copy(STEP_ROW + k, s2x.at[k], h2x.at[k], to_p), has_p, has_m)
        else:
            rows = (copy(STEP_ROW + k, s2x.at[k], h2x.at[k], to_m), has_m, has_p)
        if k in (0, 1):
            columns = (copy(STEP_COL + k, s2y.at[k], h2y.at[k], to_e), east, west)
        else:
            columns = (copy(STEP_COL + k, s2y.at[k], h2y.at[k], to_w), west, east)
        for c, sends, receives in (rows, columns):
            start(c, sends)
            second.append((c, sends, receives))

    over_y = [[], [], [], []]
    stores = []
    for k in range(4):
        for c, _, receives in second[2 * k:2 * k + 2]:
            wait_recv(c, receives)
        transport(k, r1, r2, h2x, None, h2y, None, False)
        block = pl.ds(16 * k, 16)
        c = pltpu.make_async_copy(r2.at[block], moved.at[block], out_sem.at[k])
        c.start()
        stores.append(c)
        for d in (2, 1, 3):
            yy = (y + d) % 4
            qq = jnp.where(odd == 1, 3 - yy, yy)
            part = r2[block, pl.ds(pl.multiple_of(qq * 8, 8), 8), :]
            ysend[k, d - 1] = encode(part.reshape(128, Y) * (1.0 / BOUND))
            c = copy(OVER_Y + 3 * k + d - 1, ysend.at[k, d - 1], yrecv.at[k, d - 1], at(zh, yy))
            c.start()
            over_y[k].append(c)

    def count(z, yy):
        return counts[z * 4 + yy].astype(F32)

    def plane_of(scalar):
        return jnp.full((8, Y), scalar, F32)

    def group(z):
        return count(z, 0) + count(z, 1) + count(z, 2) + count(z, 3)

    mine, across = group(zh), [group(p) for p in pair]
    everyone = group(0) + group(1) + group(2) + group(3)
    inverse_all = 1.0 / plane_of(everyone)
    inverse_mine = (1.0 / BOUND) / plane_of(mine)

    def scaled(part, factor):
        return (part.reshape(16, 8, Y) * factor).reshape(128, Y)

    over_z = [[None, None] for _ in range(4)]
    for k in range(4):
        block = pl.ds(16 * k, 16)
        part = r2[block, pl.ds(pl.multiple_of(q * 8, 8), 8), :].reshape(128, Y) * count(zh, y)
        for c, d in zip(over_y[k], (2, 1, 3)):
            c.wait_recv()
            part = part + decode(yrecv[k, d - 1]) * count(zh, (y + 4 - d) % 4)
        zsend[k, 0] = encode(scaled(part, inverse_mine))
        c = copy(OVER_Z + 2 * k, zsend.at[k, 0], zrecv.at[k, 0], at(pair[k % 2], y))
        c.start()
        over_z[k][0] = c

    wait_recv(first[4][0], first[4][2])
    wait_recv(first[5][0], first[5][2])

    @pl.when(low)
    def _():
        up_row[...] = hv_m[...]

    @pl.when(q > 0)
    def _():
        up_row[...] = val.reshape(H * X, Y)[pl.ds(16 * X + q * 8 - 1, 32, stride=X), :]

    @pl.when(high)
    def _():
        down_row[...] = hv_p[...]

    @pl.when(q < 3)
    def _():
        down_row[0:16, :] = val.reshape(H * X, Y)[pl.ds(q * 8 + 8, 16, stride=X), :]
        down_row[16:32, :] = val.reshape(H * X, Y)[pl.ds(48 * X + q * 8 + 8, 16, stride=X), :]

    wide_rows = pl.ds(pl.multiple_of(q * 8, 8), 8)
    w_rows = [weights[i, wide_rows, :] for i in range(4)]
    keep_rows = keep[wide_rows, :]
    kf_high, kf_low = split_left(kf[...])
    lane_c = lax.broadcasted_iota(I32, (64, 2 * Y), 1)
    kb = jnp.concatenate([kf_high, kf_low], axis=1)
    cf[:, 0:64] = coupling[...]
    cf[:, 64:128] = coupling[...]
    cf_high, cf_low = split_left(cf[...])
    cb = jnp.concatenate([cf_high, cf_low], axis=1)

    def reply(rows, before, after, first_column, last_column, indices):
        lowest_of, columns = [], []
        for i in indices:
            v = rows[i]
            prior = rows[i - 1][16:48, :] if i > 0 else before
            if i < 7:
                later = (rows[i + 1][0:16, :], rows[i + 1][48:64, :])
            else:
                later = (after[0:16, :], after[16:32, :])
            lane_of = lax.broadcasted_iota(I32, (32, Y), 1)
            north = jnp.where(lane_of == Y - 1, pltpu.roll(last_column, Y - 1 - i, 1), pltpu.roll(v[0:32, :], Y - 1, 1))
            west_column = pltpu.roll(first_column, Y - i, 1) if i else first_column
            south = jnp.where(lane_of == 0, west_column, pltpu.roll(v[32:64, :], 1, 1))
            moves = []
            for k in range(4):
                part = slice(16 * k, 16 * k + 16)
                vk = v[part, :]
                xn = (later[0], prior[0:16, :], prior[16:32, :], later[1])[k]
                yn = (north[0:16, :], north[16:32, :], south[0:16, :], south[16:32, :])[k]
                wx = w_rows[0 if k in (0, 3) else 1][i:i + 1, :]
                wy = w_rows[2 if k in (0, 1) else 3][i:i + 1, :]
                moves.append(vk + axt[part, :] * (wx * (xn - vk)) + ayt[part, :] * (wy * (yn - vk)))
            moves = jnp.concatenate(moves, axis=0)
            lowest = jnp.min(moves, axis=0, keepdims=True)
            lowest_of.append(lowest)
            columns.append(jnp.exp((lowest - moves) * 10.0))
        summed = jnp.dot(cb, widen(jnp.concatenate(columns, axis=1)), preferred_element_type=F32)
        logs = jnp.log(summed) * 0.1
        return [lowest_of[n] - logs[:, n * Y:(n + 1) * Y] for n in range(len(indices))]

    from_start = reply(own, up_row[...], down_row[...], hy_m[32:64, :], hy_p[32:64, :], range(8))
    for i in range(8):
        base[i] = from_start[i]

    lower = [jnp.full((8, Y), zh, I32) < jnp.full((8, Y), p, I32) for p in pair]

    def merge(k, stage, partner, weight_own, weight_other):
        a = decode(zsend[k, stage]).reshape(16, 8, Y) * weight_own
        b = decode(zrecv[k, stage]).reshape(16, 8, Y) * weight_other
        is_low = lower[partner]
        return jnp.where(is_low, a, b) + jnp.where(is_low, b, a)

    for k in range(4):
        p = k % 2
        over_z[k][0].wait_recv()
        both = merge(k, 0, p, mine, across[p])
        factor = (1.0 / BOUND) / plane_of(mine + across[p])
        zsend[k, 1] = encode((both * factor).reshape(128, Y))
        c = copy(OVER_Z + 2 * k + 1, zsend.at[k, 1], zrecv.at[k, 1], at(pair[1 - p], y))
        c.start()
        over_z[k][1] = c
    for k in range(4):
        p = k % 2
        over_z[k][1].wait_recv()
        here = mine + across[p]
        mixed = merge(k, 1, 1 - p, here, everyone - here) * inverse_all
        total[pl.ds(128 * k, 128), :] = mixed.reshape(128, Y)

    mixed_rows = jnp.concatenate([total[pl.ds(i, H, stride=8), :] for i in range(8)], axis=1)
    running = 0.5 + 0.5 * jnp.dot(kb, widen(mixed_rows), preferred_element_type=F32)
    cost = [running[:, i * Y:(i + 1) * Y] for i in range(8)]
    once = [(cost[i] + base[i]) * keep_rows[i:i + 1, :] for i in range(8)]

    sr_p[...] = once[7][16:48, :]
    sr_m[0:16, :] = once[0][0:16, :]
    sr_m[16:32, :] = once[0][48:64, :]
    sc_p[...] = pack_values(once, 32, True)
    sc_m[...] = pack_values(once, 0, False)
    edges = (
        (copy(REPLY, sr_p, hr_m, near_down), has_down, has_up),
        (copy(REPLY + 1, sr_m, hr_p, near_up), has_up, has_down),
        (copy(REPLY + 2, sc_p, hc_m, to_e), east, west),
        (copy(REPLY + 3, sc_m, hc_p, to_w), west, east),
    )
    for c, sends, _ in edges:
        start(c, sends)
    for c, _, receives in edges:
        wait_recv(c, receives)

    out_rows = out.reshape(H * X, Y)

    def unpack(codes, qq, half):
        scale = codes[256:257, :].astype(F32) * (0.125 / 32767.0)
        for n in range(4):
            v = codes[64 * n:64 * n + 64, :].astype(F32) * scale
            out_rows[pl.ds(qq * 8 + 4 * half + n, H, stride=X), :] = v

    gathers = []
    for half in range(2):
        indices = range(4 * half, 4 * half + 4)
        twice = reply(once, hr_m[...], hr_p[...], hc_m[...], hc_p[...], indices)
        twice = [(cost[i] + t) * keep_rows[i:i + 1, :] for i, t in zip(indices, twice)]
        top = jnp.max(jnp.abs(jnp.concatenate(twice, axis=0)), axis=0, keepdims=True)
        eighths = (top * 8.0).astype(I32) + 1
        inverse = (32767.0 * 8.0) / eighths.astype(F32)
        for n in range(4):
            code = (twice[n] * inverse + 32768.5).astype(I32) - 32768
            gsend[half, pl.ds(64 * n, 64), :] = code.astype(I16)
        gsend[half, pl.ds(256, 16), :] = jnp.broadcast_to(eighths, (16, Y)).astype(I16)
        for d in (2, 1, 3):
            c = copy(GATHER + 3 * half + d - 1, gsend.at[half], grecv.at[half, d - 1], at(zh, (y + d) % 4))
            c.start()
            gathers.append((c, half, d))
    for half in range(2):
        unpack(gsend[half].astype(I32), q, half)
    for c, half, d in gathers:
        c.wait_recv()
        yy = (y + 4 - d) % 4
        unpack(grecv[half, d - 1].astype(I32), jnp.where(odd == 1, 3 - yy, yy), half)
    c = pltpu.make_async_copy(out, values, out_sem.at[4])
    c.start()
    stores.append(c)

    for c, sends, _ in (*first, *second, *edges):
        wait_send(c, sends)
    for k in range(4):
        for c in (*over_y[k], *over_z[k]):
            c.wait_send()
    for c, _, _ in gathers:
        c.wait_send()
    for c in stores:
        c.wait()


def shards(density, turn_rate, value_init, labels, counts, kernel_matrix):
    along_x, along_y, coupling = tables()
    vmem = lambda *shape: pltpu.VMEM(shape, F32)
    anywhere = pl.BlockSpec(memory_space=pl.ANY)
    scratch = [
        vmem(H, X, Y), pltpu.VMEM((H, X, Y), BF16), vmem(H, X, Y), pltpu.VMEM((X, Y), I32), vmem(H, Y), vmem(H, Y),
        vmem(H, H), vmem(H, H),
        vmem(40, Y), vmem(40, Y), vmem(64, Y), vmem(64, Y), vmem(32, Y), vmem(32, Y),
        vmem(40, Y), vmem(40, Y), vmem(64, Y), vmem(64, Y), vmem(32, Y), vmem(32, Y),
        vmem(H, X, Y), vmem(H, X, Y), vmem(4, 16, Y), vmem(4, X, Y), vmem(4, 16, Y), vmem(4, X, Y), vmem(4, X, Y),
        vmem(X, Y),
        pltpu.VMEM((4, 3, 128, Y), I16), pltpu.VMEM((4, 3, 128, Y), I16),
        pltpu.VMEM((4, 2, 128, Y), I16), pltpu.VMEM((4, 2, 128, Y), I16), vmem(512, Y), vmem(8, H, Y),
        vmem(32, Y), vmem(32, Y), vmem(8, Y), vmem(H, 128), vmem(H, 128),
        *[vmem(32, Y) for _ in range(8)],
        pltpu.VMEM((2, 272, Y), I16), pltpu.VMEM((2, 3, 272, Y), I16), vmem(H, X, Y),
        pltpu.SemaphoreType.DMA((8,)), pltpu.SemaphoreType.DMA((5,)),
        pltpu.SemaphoreType.DMA((COPIES,)), pltpu.SemaphoreType.DMA((COPIES,)),
    ]
    moved, values = pl.pallas_call(
        kernel,
        out_shape=(jax.ShapeDtypeStruct((H, X, Y), F32), jax.ShapeDtypeStruct((H, X, Y), F32)),
        in_specs=[pl.BlockSpec(memory_space=pltpu.SMEM)] + [anywhere] * 8,
        out_specs=(anywhere, anywhere),
        scratch_shapes=scratch,
        compiler_params=pltpu.CompilerParams(
            collective_id=1, has_side_effects=True, vmem_limit_bytes=40 * 1024 * 1024
        ),
        name="play",
    )(
        counts, density[0], turn_rate[0], value_init, labels,
        jnp.asarray(along_x), jnp.asarray(along_y), jnp.asarray(coupling), kernel_matrix,
    )
    return moved[None], values


def solution(mesh):
    placed = (
        P("member", None, "gx", "gy"),
        P("member", None, "gx", "gy"),
        P(None, "gx", "gy"),
        P("gx", "gy"),
        P(),
        P(),
    )
    return jax.shard_map(
        shards,
        mesh=mesh,
        in_specs=placed,
        out_specs=(P("member", None, "gx", "gy"), P(None, "gx", "gy")),
        check_vma=False,
    )
```

```python
import jax
import jax.numpy as jnp
import numpy as np
from jax import lax
from jax.experimental import pallas as pl
from jax.experimental.pallas import tpu as pltpu
from jax.sharding import PartitionSpec as P

MESH = pl.DeviceIdType.MESH
F32 = jnp.float32
BF16 = jnp.bfloat16
I16 = jnp.int16
I32 = jnp.int32

H, X, Y = 64, 32, 128
SPEED = 0.55
BOUND = 9.5

ROW_UP, ROW_DOWN, COL_UP, COL_DOWN, VAL_UP, VAL_DOWN = range(6)
CHUNK = 8
CHUNKS = H // CHUNK
ROWS = 8 * CHUNK
STEP_ROW, STEP_COL, OVER_Y = 6, 10, 14
OVER_Z = OVER_Y + 3 * CHUNKS
REPLY = OVER_Z + 2 * CHUNKS
GATHER = REPLY + 4
PIECES = 4
SPAN = 8 // PIECES
MARK = H * SPAN
COPIES = GATHER + 3 * PIECES


def tables():
    angles = np.arange(H, dtype=np.float32) * np.float32(2.0 * np.pi / H)
    along_x = np.abs(SPEED * np.cos(angles)).astype(np.float32)
    along_y = np.abs(SPEED * np.sin(angles)).astype(np.float32)
    spread = angles[:, None] - angles[None, :]
    coupling = np.exp(-5.0 * (1.0 - np.cos(spread.astype(np.float64)))).astype(np.float32)
    wide = lambda v: np.ascontiguousarray(np.broadcast_to(v[:, None], (H, Y)))
    return wide(along_x), wide(along_y), coupling


def encode(x):
    root = jnp.sqrt(jnp.maximum(x, 0.0)) * 65535.0 + 0.5
    return (root.astype(I32) - 32768).astype(I16)


def decode(code):
    root = code.astype(I32).astype(F32) + 32768.0
    return root * root * (BOUND / (65535.0 * 65535.0))


def split_left(m):
    high = m.astype(BF16)
    low = (m - high.astype(F32)).astype(BF16)
    return high, low


def widen(m):
    high, low = split_left(m)
    return jnp.concatenate([high, low, high, low], axis=0)


def kernel(
    counts_hbm, density, turn_hbm, value_hbm, labels_hbm, ax_hbm, ay_hbm, coupling_hbm, kernel_hbm,
    r2, out,
    r0, turn, val, labels, axt, ayt, coupling, kern,
    sx_m, sx_p, sy_m, sy_p, sv_m, sv_p, hx_m, hx_p, hy_m, hy_p, hv_m, hv_p,
    r1, s2x, s2y, h2x, h2y, weights, keep,
    ysend, yrecv, zsend, zrecv, total, base,
    up_row, down_row, cs, kf, cf,
    sr_m, sr_p, sc_m, sc_p, hr_m, hr_p, hc_m, hc_p,
    gsend, grecv,
    counts, load_sem, ss, rs,
):
    member = lax.axis_index("member")
    gx = lax.axis_index("gx")
    gy = lax.axis_index("gy")
    zh, y = member // 4, member % 4
    odd = gx % 2
    q = jnp.where(odd == 1, 3 - y, y)
    turn_sign = jnp.where(odd == 1, 3, 1)

    def at(z, yy):
        return {"member": z * 4 + yy}

    pair = (jnp.where(zh % 2 == 0, zh + 1, zh - 1), 3 - zh)

    barrier = pltpu.get_barrier_semaphore()
    greeted = [at(zh, (y + d) % 4) for d in (1, 2, 3)] + [at(p, y) for p in pair]
    greeted += [{"gy": (gy + d) % 4} for d in (1, 3)]

    def greet(target):
        pl.semaphore_signal(barrier, inc=1, device_id=target, device_id_type=MESH)

    has_m, has_p = gx > 0, gx < 7
    west, east = gy > 0, gy < 3
    to_m, to_p = {"gx": (gx + 7) % 8}, {"gx": (gx + 1) % 8}
    to_w, to_e = {"gy": (gy + 3) % 4}, {"gy": (gy + 1) % 4}
    pl.when(has_m)(lambda: greet(to_m))
    pl.when(has_p)(lambda: greet(to_p))
    for target in greeted:
        greet(target)

    loads = [
        pltpu.make_async_copy(src, dst, load_sem.at[i])
        for i, (src, dst) in enumerate((
            (density, r0), (labels_hbm, labels), (value_hbm, val), (turn_hbm, turn), (ax_hbm, axt), (ay_hbm, ayt),
            (coupling_hbm, coupling), (kernel_hbm, kern),
            (counts_hbm, counts),
        ))
    ]
    for c in loads:
        c.start()

    def copy(i, src, dst, target):
        return pltpu.make_async_remote_copy(
            src_ref=src, dst_ref=dst, send_sem=ss.at[i], recv_sem=rs.at[i], device_id=target, device_id_type=MESH
        )

    lane = lax.broadcasted_iota(I32, (X, Y), 1)
    row = lax.broadcasted_iota(I32, (X, Y), 0)
    lane_h = lax.broadcasted_iota(I32, (32, Y), 1)

    def shift_x(r, halo, k):
        if k in (0, 3):
            return jnp.where(row == 0, halo, pltpu.roll(r, 1, 0))
        return jnp.where(row == X - 1, halo, pltpu.roll(r, X - 1, 0))

    def shift_y(r, halo, position, k):
        if k in (0, 1):
            moved_halo = pltpu.roll(halo, lax.rem(Y - position, Y), 1)
            return jnp.where(lane == 0, moved_halo, pltpu.roll(r, 1, 1))
        moved_halo = pltpu.roll(halo, Y - 1 - position, 1)
        return jnp.where(lane == Y - 1, moved_halo, pltpu.roll(r, Y - 1, 1))

    def pack_column(acc, r, position, k):
        shift = position + 1 if k in (0, 1) else position
        return jnp.where(lane == position, pltpu.roll(r, shift, 1), acc)

    loads[0].wait()
    loads[1].wait()
    opened = jnp.where(labels[...] != 1, 1.0, 0.0).astype(F32)
    keep[...] = jnp.where(labels[...] == 2, 0.0, 1.0).astype(F32)
    zero_plane = jnp.zeros((X, Y), F32)

    def rows_of(ref, h0, n, x):
        return ref.reshape(H * X, Y)[pl.ds(h0 * X + x, n, stride=X), :]

    sx_p[0:16, :] = rows_of(r0, 0, 16, X - 1)
    sx_p[16:32, :] = rows_of(r0, 48, 16, X - 1)
    sx_p[32:40, :] = jnp.broadcast_to(opened[X - 1:X, :], (8, Y))
    sx_m[0:32, :] = rows_of(r0, 16, 32, 0)
    sx_m[32:40, :] = jnp.broadcast_to(opened[0:1, :], (8, Y))

    for k0, dst, shift in ((0, sy_p, 65), (2, sy_m, 64)):
        def pack(j, acc, k0=k0):
            return pack_column(acc, r0[k0 * 16 + j], j, k0)
        acc = lax.fori_loop(0, 32, pack, zero_plane, unroll=32)
        dst[0:32, :] = jnp.where(lane == 64, pltpu.roll(opened, shift, 1), acc)

    def value_row(i):
        return val.reshape(H * X, Y)[pl.ds(q * 8 + i, H, stride=X), :]

    def pack_values(rows, headings, side):
        acc = jnp.zeros((32, Y), F32)
        for i in range(8):
            part = rows[i][headings:headings + 32, :]
            shift = i + 1 if side else i
            acc = jnp.where(lane_h == i, pltpu.roll(part, shift, 1) if shift else part, acc)
        return acc

    loads[2].wait()
    own = [value_row(i) for i in range(8)]
    sy_p[32:64, :] = pack_values(own, 32, True)
    sy_m[32:64, :] = pack_values(own, 0, False)
    sv_p[...] = own[7][16:48, :]
    sv_m[0:16, :] = own[0][0:16, :]
    sv_m[16:32, :] = own[0][48:64, :]

    @pl.when(gx == 0)
    def _():
        hx_m[...] = jnp.zeros((40, Y), F32)
        hv_m[...] = jnp.zeros((32, Y), F32)
        h2x[0] = jnp.zeros((16, Y), F32)
        h2x[3] = jnp.zeros((16, Y), F32)

    @pl.when(gx == 7)
    def _():
        hx_p[...] = jnp.zeros((40, Y), F32)
        hv_p[...] = jnp.zeros((32, Y), F32)
        h2x[1] = jnp.zeros((16, Y), F32)
        h2x[2] = jnp.zeros((16, Y), F32)

    @pl.when(gy == 0)
    def _():
        hy_m[...] = jnp.zeros((64, Y), F32)
        hc_m[...] = jnp.zeros((32, Y), F32)
        h2y[0] = zero_plane
        h2y[1] = zero_plane

    @pl.when(gy == 3)
    def _():
        hy_p[...] = jnp.zeros((64, Y), F32)
        hc_p[...] = jnp.zeros((32, Y), F32)
        h2y[2] = zero_plane
        h2y[3] = zero_plane

    low, high = q == 0, q == 3
    near_up = {"member": zh * 4 + jnp.where(low, y, (y + 4 - turn_sign) % 4), "gx": jnp.where(low, (gx + 7) % 8, gx)}
    near_down = {"member": zh * 4 + jnp.where(high, y, (y + turn_sign) % 4), "gx": jnp.where(high, (gx + 1) % 8, gx)}
    has_up, has_down = jnp.logical_or(q > 0, has_m), jnp.logical_or(q < 3, has_p)

    @pl.when(jnp.logical_not(has_up))
    def _():
        hr_m[...] = jnp.zeros((32, Y), F32)

    @pl.when(jnp.logical_not(has_down))
    def _():
        hr_p[...] = jnp.zeros((32, Y), F32)

    first = (
        (copy(ROW_DOWN, sx_p, hx_m, to_p), has_p, has_m),
        (copy(ROW_UP, sx_m, hx_p, to_m), has_m, has_p),
        (copy(COL_DOWN, sy_p, hy_m, to_e), east, west),
        (copy(COL_UP, sy_m, hy_p, to_w), west, east),
        (copy(VAL_DOWN, sv_p, hv_m, to_p), jnp.logical_and(high, has_p), jnp.logical_and(low, has_m)),
        (copy(VAL_UP, sv_m, hv_p, to_m), jnp.logical_and(low, has_m), jnp.logical_and(high, has_p)),
    )

    started, landed = [], set()

    def guarded(condition, act):
        if condition is True:
            act()
        else:
            pl.when(condition)(act)

    def launch(c, sends=True, receives=True):
        guarded(sends, c.start)
        started.append((c, sends, receives))
        return len(started) - 1

    def land(n):
        c, _, receives = started[n]
        guarded(receives, c.wait_recv)
        landed.add(n)

    def finish_all():
        for n, (c, sends, _) in enumerate(started):
            if n not in landed:
                land(n)
            guarded(sends, c.wait_send)

    pl.semaphore_wait(barrier, len(greeted) + has_m.astype(I32) + has_p.astype(I32))
    first = [launch(*c) for c in first]
    for c in loads[3:]:
        c.wait()
    kf[:, 0:64] = kern[...]
    kf[:, 64:128] = kern[...]
    for n in first[:4]:
        land(n)

    open_p = jnp.where(row == X - 1, hx_p[32:33, :], pltpu.roll(opened, X - 1, 0))
    open_m = jnp.where(row == 0, hx_m[32:33, :], pltpu.roll(opened, 1, 0))
    open_e = jnp.where(lane == Y - 1, pltpu.roll(hy_p[0:32, :], 63, 1), pltpu.roll(opened, Y - 1, 1))
    open_w = jnp.where(lane == 0, pltpu.roll(hy_m[0:32, :], 64, 1), pltpu.roll(opened, 1, 1))
    weights[0] = opened * open_p
    weights[1] = opened * open_m
    weights[2] = opened * open_e
    weights[3] = opened * open_w

    def transport(k, src, dst, halo_x, x_at, halo_y, y_at, pack):
        out_x, in_x = (0, 1) if k in (0, 3) else (1, 0)
        out_y, in_y = (2, 3) if k in (0, 1) else (3, 2)
        wox, wix, woy, wiy = weights[out_x], weights[in_x], weights[out_y], weights[in_y]
        kept = keep[...]
        columns = halo_y[0:32, :] if y_at is not None else halo_y[k]
        h0 = 16 * k
        y_from = 0 if y_at is None else y_at

        def turns(h):
            r = src[h]
            t = turn[h].astype(F32)
            up = jnp.maximum(t, 0.0) * r
            return r, up, up - t * r

        def start_of(j):
            h = h0 + j
            r, up, down = turns(h)
            ax = axt[pl.ds(h, 1), :]
            ay = ayt[pl.ds(h, 1), :]
            hx = halo_x[pl.ds(x_at + j, 1), :] if x_at is not None else halo_x[k, pl.ds(j, 1), :]
            xn = shift_x(r, hx, k)
            yn = shift_y(r, columns, y_from + j, k)
            s = r - up - down + ax * (wix * xn - wox * r) + ay * (wiy * yn - woy * r)
            return s, up, down

        _, up_before, _ = turns((h0 + 63) % 64)
        s, up, _ = start_of(0)
        carry = (s + up_before, up, zero_plane)

        def finish(j, partial, down, acc):
            new = (partial + down) * kept
            dst[h0 + j] = new
            return pack_column(acc, new, j, k) if pack else acc

        def body(j, carry):
            partial, up_last, acc = carry
            s, up, down = start_of(j)
            acc = finish(j - 1, partial, down, acc)
            return s + up_last, up, acc

        partial, _, acc = lax.fori_loop(1, 16, body, carry, unroll=15)
        _, _, down = turns((h0 + 16) % 64)
        return finish(15, partial, down, acc)

    second = []
    for k in range(4):
        halo_x, x_at = ((hx_m, 0), (hx_p, 0), (hx_p, 16), (hx_m, 16))[k]
        halo_y, y_at = ((hy_m, 0), (hy_m, 16), (hy_p, 0), (hy_p, 16))[k]
        acc = transport(k, r0, r1, halo_x, x_at, halo_y, y_at, True)
        s2y[k] = acc
        s2x[k] = rows_of(r1, 16 * k, 16, X - 1 if k in (0, 3) else 0)
        if k in (0, 3):
            rows = (copy(STEP_ROW + k, s2x.at[k], h2x.at[k], to_p), has_p, has_m)
        else:
            rows = (copy(STEP_ROW + k, s2x.at[k], h2x.at[k], to_m), has_m, has_p)
        if k in (0, 1):
            columns = (copy(STEP_COL + k, s2y.at[k], h2y.at[k], to_e), east, west)
        else:
            columns = (copy(STEP_COL + k, s2y.at[k], h2y.at[k], to_w), west, east)
        second += [launch(*rows), launch(*columns)]

    over_y = [[] for _ in range(CHUNKS)]
    for k in range(4):
        for n in second[2 * k:2 * k + 2]:
            land(n)
        transport(k, r1, r2, h2x, None, h2y, None, False)
        for c in range(k * CHUNKS // 4, (k + 1) * CHUNKS // 4):
            for d in (2, 1, 3):
                yy = (y + d) % 4
                qq = jnp.where(odd == 1, 3 - yy, yy)
                part = r2[pl.ds(CHUNK * c, CHUNK), pl.ds(pl.multiple_of(qq * 8, 8), 8), :]
                ysend[c, d - 1] = encode(part.reshape(ROWS, Y) * (1.0 / BOUND))
                there = copy(OVER_Y + 3 * c + d - 1, ysend.at[c, d - 1], yrecv.at[c, d - 1], at(zh, yy))
                over_y[c].append(launch(there))

    def count(z, yy):
        return counts[z * 4 + yy].astype(F32)

    def plane_of(scalar):
        return jnp.full((8, Y), scalar, F32)

    def group(z):
        return count(z, 0) + count(z, 1) + count(z, 2) + count(z, 3)

    mine, across = group(zh), [group(p) for p in pair]
    everyone = group(0) + group(1) + group(2) + group(3)
    inverse_all = 1.0 / plane_of(everyone)
    inverse_mine = (1.0 / BOUND) / plane_of(mine)

    def scaled(part, factor):
        return (part.reshape(CHUNK, 8, Y) * factor).reshape(ROWS, Y)

    over_z = [[None, None] for _ in range(CHUNKS)]
    for c in range(CHUNKS):
        block = pl.ds(CHUNK * c, CHUNK)
        part = r2[block, pl.ds(pl.multiple_of(q * 8, 8), 8), :].reshape(ROWS, Y) * count(zh, y)
        for n, d in zip(over_y[c], (2, 1, 3)):
            land(n)
            part = part + decode(yrecv[c, d - 1]) * count(zh, (y + 4 - d) % 4)
        zsend[c, 0] = encode(scaled(part, inverse_mine))
        over_z[c][0] = launch(copy(OVER_Z + 2 * c, zsend.at[c, 0], zrecv.at[c, 0], at(pair[c % 2], y)))

    land(first[4])
    land(first[5])

    @pl.when(low)
    def _():
        up_row[...] = hv_m[...]

    @pl.when(q > 0)
    def _():
        up_row[...] = val.reshape(H * X, Y)[pl.ds(16 * X + q * 8 - 1, 32, stride=X), :]

    @pl.when(high)
    def _():
        down_row[...] = hv_p[...]

    @pl.when(q < 3)
    def _():
        down_row[0:16, :] = val.reshape(H * X, Y)[pl.ds(q * 8 + 8, 16, stride=X), :]
        down_row[16:32, :] = val.reshape(H * X, Y)[pl.ds(48 * X + q * 8 + 8, 16, stride=X), :]

    wide_rows = pl.ds(pl.multiple_of(q * 8, 8), 8)
    w_rows = [weights[i, wide_rows, :] for i in range(4)]
    keep_rows = keep[wide_rows, :]
    kf_high, kf_low = split_left(kf[...])
    lane_c = lax.broadcasted_iota(I32, (64, 2 * Y), 1)
    kb = jnp.concatenate([kf_high, kf_low], axis=1)
    cf[:, 0:64] = coupling[...]
    cf[:, 64:128] = coupling[...]
    cf_high, cf_low = split_left(cf[...])
    cb = jnp.concatenate([cf_high, cf_low], axis=1)

    def reply(rows, before, after, first_column, last_column, indices):
        lowest_of, columns = [], []
        for i in indices:
            v = rows[i]
            prior = rows[i - 1][16:48, :] if i > 0 else before
            if i < 7:
                later = (rows[i + 1][0:16, :], rows[i + 1][48:64, :])
            else:
                later = (after[0:16, :], after[16:32, :])
            lane_of = lax.broadcasted_iota(I32, (32, Y), 1)
            north = jnp.where(lane_of == Y - 1, pltpu.roll(last_column, Y - 1 - i, 1), pltpu.roll(v[0:32, :], Y - 1, 1))
            west_column = pltpu.roll(first_column, Y - i, 1) if i else first_column
            south = jnp.where(lane_of == 0, west_column, pltpu.roll(v[32:64, :], 1, 1))
            moves = []
            for k in range(4):
                part = slice(16 * k, 16 * k + 16)
                vk = v[part, :]
                xn = (later[0], prior[0:16, :], prior[16:32, :], later[1])[k]
                yn = (north[0:16, :], north[16:32, :], south[0:16, :], south[16:32, :])[k]
                wx = w_rows[0 if k in (0, 3) else 1][i:i + 1, :]
                wy = w_rows[2 if k in (0, 1) else 3][i:i + 1, :]
                moves.append(vk + axt[part, :] * (wx * (xn - vk)) + ayt[part, :] * (wy * (yn - vk)))
            moves = jnp.concatenate(moves, axis=0)
            lowest = jnp.min(moves, axis=0, keepdims=True)
            lowest_of.append(lowest)
            columns.append(jnp.exp((lowest - moves) * 10.0))
        summed = jnp.dot(cb, widen(jnp.concatenate(columns, axis=1)), preferred_element_type=F32)
        logs = jnp.log(summed) * 0.1
        return [lowest_of[n] - logs[:, n * Y:(n + 1) * Y] for n in range(len(indices))]

    from_start = reply(own, up_row[...], down_row[...], hy_m[32:64, :], hy_p[32:64, :], range(8))
    for i in range(8):
        base[i] = from_start[i]

    lower = [jnp.full((8, Y), zh, I32) < jnp.full((8, Y), p, I32) for p in pair]

    def merge(c, stage, partner, weight_own, weight_other):
        a = decode(zsend[c, stage]).reshape(CHUNK, 8, Y) * weight_own
        b = decode(zrecv[c, stage]).reshape(CHUNK, 8, Y) * weight_other
        is_low = lower[partner]
        return jnp.where(is_low, a, b) + jnp.where(is_low, b, a)

    factors = [(1.0 / BOUND) / plane_of(mine + across[p]) for p in range(2)]
    for c in range(CHUNKS):
        p = c % 2
        land(over_z[c][0])
        both = merge(c, 0, p, mine, across[p])
        zsend[c, 1] = encode((both * factors[p]).reshape(ROWS, Y))
        over_z[c][1] = launch(copy(OVER_Z + 2 * c + 1, zsend.at[c, 1], zrecv.at[c, 1], at(pair[1 - p], y)))
    for c in range(CHUNKS):
        p = c % 2
        land(over_z[c][1])
        here = mine + across[p]
        mixed = merge(c, 1, 1 - p, here, everyone - here) * inverse_all
        total[pl.ds(ROWS * c, ROWS), :] = mixed.reshape(ROWS, Y)

    mixed_rows = jnp.concatenate([total[pl.ds(i, H, stride=8), :] for i in range(8)], axis=1)
    running = 0.5 + 0.5 * jnp.dot(kb, widen(mixed_rows), preferred_element_type=F32)
    cost = [running[:, i * Y:(i + 1) * Y] for i in range(8)]
    once = [(cost[i] + base[i]) * keep_rows[i:i + 1, :] for i in range(8)]

    sr_p[...] = once[7][16:48, :]
    sr_m[0:16, :] = once[0][0:16, :]
    sr_m[16:32, :] = once[0][48:64, :]
    sc_p[...] = pack_values(once, 32, True)
    sc_m[...] = pack_values(once, 0, False)
    edges = (
        (copy(REPLY, sr_p, hr_m, near_down), has_down, has_up),
        (copy(REPLY + 1, sr_m, hr_p, near_up), has_up, has_down),
        (copy(REPLY + 2, sc_p, hc_m, to_e), east, west),
        (copy(REPLY + 3, sc_m, hc_p, to_w), west, east),
    )
    edges = [launch(*c) for c in edges]
    for n in edges:
        land(n)

    out_rows = out.reshape(H * X, Y)

    def unpack(codes, qq, piece):
        scale = codes[MARK:MARK + 1, :].astype(F32) * (0.125 / 32767.0)
        for n in range(SPAN):
            v = codes[H * n:H * n + H, :].astype(F32) * scale
            out_rows[pl.ds(qq * 8 + SPAN * piece + n, H, stride=X), :] = v

    gathers = []
    for piece in range(PIECES):
        indices = range(SPAN * piece, SPAN * piece + SPAN)
        twice = reply(once, hr_m[...], hr_p[...], hc_m[...], hc_p[...], indices)
        twice = [(cost[i] + t) * keep_rows[i:i + 1, :] for i, t in zip(indices, twice)]
        top = jnp.max(jnp.abs(jnp.concatenate(twice, axis=0)), axis=0, keepdims=True)
        eighths = (top * 8.0).astype(I32) + 1
        inverse = (32767.0 * 8.0) / eighths.astype(F32)
        for n in range(SPAN):
            code = (twice[n] * inverse + 32768.5).astype(I32) - 32768
            gsend[piece, pl.ds(H * n, H), :] = code.astype(I16)
        gsend[piece, pl.ds(MARK, 16), :] = jnp.broadcast_to(eighths, (16, Y)).astype(I16)
        for d in (2, 1, 3):
            there = copy(GATHER + 3 * piece + d - 1, gsend.at[piece], grecv.at[piece, d - 1], at(zh, (y + d) % 4))
            gathers.append((launch(there), piece, d))
    for piece in range(PIECES):
        unpack(gsend[piece].astype(I32), q, piece)
    for n, piece, d in gathers:
        land(n)
        yy = (y + 4 - d) % 4
        unpack(grecv[piece, d - 1].astype(I32), jnp.where(odd == 1, 3 - yy, yy), piece)
    finish_all()


def write_out(moved, values, moved_out, values_out, sems):
    copies = [
        pltpu.make_async_copy(src, dst, sems.at[i])
        for i, (src, dst) in enumerate(((moved, moved_out), (values, values_out)))
    ]
    for c in copies:
        c.start()
    for c in copies:
        c.wait()


def shards(density, turn_rate, value_init, labels, counts, kernel_matrix):
    along_x, along_y, coupling = tables()
    vmem = lambda *shape: pltpu.VMEM(shape, F32)
    in_hbm = pl.BlockSpec(memory_space=pltpu.HBM)
    scratch = [
        vmem(H, X, Y), pltpu.VMEM((H, X, Y), BF16), vmem(H, X, Y), pltpu.VMEM((X, Y), I32), vmem(H, Y), vmem(H, Y),
        vmem(H, H), vmem(H, H),
        vmem(40, Y), vmem(40, Y), vmem(64, Y), vmem(64, Y), vmem(32, Y), vmem(32, Y),
        vmem(40, Y), vmem(40, Y), vmem(64, Y), vmem(64, Y), vmem(32, Y), vmem(32, Y),
        vmem(H, X, Y), vmem(4, 16, Y), vmem(4, X, Y), vmem(4, 16, Y), vmem(4, X, Y), vmem(4, X, Y),
        vmem(X, Y),
        pltpu.VMEM((CHUNKS, 3, ROWS, Y), I16), pltpu.VMEM((CHUNKS, 3, ROWS, Y), I16),
        pltpu.VMEM((CHUNKS, 2, ROWS, Y), I16), pltpu.VMEM((CHUNKS, 2, ROWS, Y), I16), vmem(512, Y), vmem(8, H, Y),
        vmem(32, Y), vmem(32, Y), vmem(8, Y), vmem(H, 128), vmem(H, 128),
        *[vmem(32, Y) for _ in range(8)],
        pltpu.VMEM((PIECES, MARK + 16, Y), I16), pltpu.VMEM((PIECES, 3, MARK + 16, Y), I16),
        pltpu.SMEM((16,), I32), pltpu.SemaphoreType.DMA((9,)),
        pltpu.SemaphoreType.DMA((COPIES,)), pltpu.SemaphoreType.DMA((COPIES,)),
    ]
    held = pltpu.VMEM((H, X, Y), F32)
    in_vmem = pl.BlockSpec(memory_space=pltpu.VMEM)
    operands = (
        counts, density[0], turn_rate[0], value_init, labels,
        jnp.asarray(along_x), jnp.asarray(along_y), jnp.asarray(coupling), kernel_matrix,
    )
    moved, values = pl.pallas_call(
        kernel,
        out_shape=(held, held),
        in_specs=[in_hbm] * 9,
        out_specs=(in_vmem, in_vmem),
        scratch_shapes=scratch,
        compiler_params=pltpu.CompilerParams(
            collective_id=1, has_side_effects=True, vmem_limit_bytes=40 * 1024 * 1024
        ),
        name="play",
    )(*[pltpu.with_memory_space_constraint(a, pltpu.HBM) for a in operands])
    whole = jax.ShapeDtypeStruct((H, X, Y), F32)
    moved, values = pl.pallas_call(
        write_out,
        out_shape=(whole, whole),
        in_specs=[in_vmem, in_vmem],
        out_specs=(in_hbm, in_hbm),
        scratch_shapes=[pltpu.SemaphoreType.DMA((2,))],
        compiler_params=pltpu.CompilerParams(vmem_limit_bytes=8 * 1024 * 1024),
        name="write",
    )(moved, values)
    return moved[None], values


def solution(mesh):
    placed = (
        P("member", None, "gx", "gy"),
        P("member", None, "gx", "gy"),
        P(None, "gx", "gy"),
        P("gx", "gy"),
        P(),
        P(),
    )
    return jax.shard_map(
        shards,
        mesh=mesh,
        in_specs=placed,
        out_specs=(P("member", None, "gx", "gy"), P(None, "gx", "gy")),
        check_vma=False,
    )
```

```python
import jax
import jax.numpy as jnp
import numpy as np
from jax import lax
from jax.experimental import pallas as pl
from jax.experimental.pallas import tpu as pltpu
from jax.sharding import PartitionSpec as P

MESH = pl.DeviceIdType.MESH
F32 = jnp.float32
BF16 = jnp.bfloat16
I16 = jnp.int16
I32 = jnp.int32

H, X, Y = 64, 32, 128
SPEED = 0.55
BOUND = 9.5

ROW_UP, ROW_DOWN, COL_UP, COL_DOWN, VAL_UP, VAL_DOWN, VALCOL_UP, VALCOL_DOWN = range(8)
CHUNK = 8
CHUNKS = H // CHUNK
ROWS = 8 * CHUNK
STEP_ROW, STEP_COL, OVER_Y = 8, 12, 16
OVER_Z = OVER_Y + 3 * CHUNKS
REPLY = OVER_Z + 2 * CHUNKS
GATHER = REPLY + 4
PIECES = 4
SPAN = 8 // PIECES
MARK = H * SPAN
COPIES = GATHER + 3 * PIECES


def tables():
    angles = np.arange(H, dtype=np.float32) * np.float32(2.0 * np.pi / H)
    along_x = np.abs(SPEED * np.cos(angles)).astype(np.float32)
    along_y = np.abs(SPEED * np.sin(angles)).astype(np.float32)
    spread = angles[:, None] - angles[None, :]
    coupling = np.exp(-5.0 * (1.0 - np.cos(spread.astype(np.float64)))).astype(np.float32)
    wide = lambda v: np.ascontiguousarray(np.broadcast_to(v[:, None], (H, Y)))
    return wide(along_x), wide(along_y), coupling


def encode(x):
    root = jnp.sqrt(jnp.maximum(x, 0.0)) * 65535.0 + 0.5
    return (root.astype(I32) - 32768).astype(I16)


def decode(code):
    root = code.astype(I32).astype(F32) + 32768.0
    return root * root * (BOUND / (65535.0 * 65535.0))


def split_left(m):
    high = m.astype(BF16)
    low = (m - high.astype(F32)).astype(BF16)
    return high, low


def widen(m):
    high, low = split_left(m)
    return jnp.concatenate([high, low, high, low], axis=0)


def kernel(
    counts_hbm, density, turn_hbm, value_hbm, labels_hbm, ax_hbm, ay_hbm, coupling_hbm, kernel_hbm,
    r2, out,
    r0, turn, val, labels, axt, ayt, coupling, kern,
    sx_m, sx_p, sy_m, sy_p, sv_m, sv_p, svc_m, svc_p, hx_m, hx_p, hy_m, hy_p, hv_m, hv_p, hvc_m, hvc_p,
    r1, s2x, s2y, h2x, h2y, weights, keep,
    ysend, yrecv, zsend, zrecv, total, base,
    up_row, down_row, cs, kf, cf,
    sr_m, sr_p, sc_m, sc_p, hr_m, hr_p, hc_m, hc_p,
    gsend, grecv,
    counts, load_sem, ss, rs,
):
    member = lax.axis_index("member")
    gx = lax.axis_index("gx")
    gy = lax.axis_index("gy")
    zh, y = member // 4, member % 4
    odd = gx % 2
    q = jnp.where(odd == 1, 3 - y, y)
    turn_sign = jnp.where(odd == 1, 3, 1)

    def at(z, yy):
        return {"member": z * 4 + yy}

    pair = (jnp.where(zh % 2 == 0, zh + 1, zh - 1), 3 - zh)

    barrier = pltpu.get_barrier_semaphore()
    greeted = [at(zh, (y + d) % 4) for d in (1, 2, 3)] + [at(p, y) for p in pair]
    greeted += [{"gy": (gy + d) % 4} for d in (1, 3)]

    def greet(target):
        pl.semaphore_signal(barrier, inc=1, device_id=target, device_id_type=MESH)

    has_m, has_p = gx > 0, gx < 7
    west, east = gy > 0, gy < 3
    to_m, to_p = {"gx": (gx + 7) % 8}, {"gx": (gx + 1) % 8}
    to_w, to_e = {"gy": (gy + 3) % 4}, {"gy": (gy + 1) % 4}
    pl.when(has_m)(lambda: greet(to_m))
    pl.when(has_p)(lambda: greet(to_p))
    for target in greeted:
        greet(target)

    loads = [
        pltpu.make_async_copy(src, dst, load_sem.at[i])
        for i, (src, dst) in enumerate((
            (density, r0), (labels_hbm, labels), (value_hbm, val), (turn_hbm, turn), (ax_hbm, axt), (ay_hbm, ayt),
            (coupling_hbm, coupling), (kernel_hbm, kern),
            (counts_hbm, counts),
        ))
    ]
    for c in loads:
        c.start()

    def copy(i, src, dst, target):
        return pltpu.make_async_remote_copy(
            src_ref=src, dst_ref=dst, send_sem=ss.at[i], recv_sem=rs.at[i], device_id=target, device_id_type=MESH
        )

    lane = lax.broadcasted_iota(I32, (X, Y), 1)
    row = lax.broadcasted_iota(I32, (X, Y), 0)
    lane_h = lax.broadcasted_iota(I32, (32, Y), 1)

    def shift_x(r, halo, k):
        if k in (0, 3):
            return jnp.where(row == 0, halo, pltpu.roll(r, 1, 0))
        return jnp.where(row == X - 1, halo, pltpu.roll(r, X - 1, 0))

    def shift_y(r, halo, position, k):
        if k in (0, 1):
            moved_halo = pltpu.roll(halo, lax.rem(Y - position, Y), 1)
            return jnp.where(lane == 0, moved_halo, pltpu.roll(r, 1, 1))
        moved_halo = pltpu.roll(halo, Y - 1 - position, 1)
        return jnp.where(lane == Y - 1, moved_halo, pltpu.roll(r, Y - 1, 1))

    def pack_column(acc, r, position, k):
        shift = position + 1 if k in (0, 1) else position
        return jnp.where(lane == position, pltpu.roll(r, shift, 1), acc)

    loads[0].wait()
    loads[1].wait()
    opened = jnp.where(labels[...] != 1, 1.0, 0.0).astype(F32)
    keep[...] = jnp.where(labels[...] == 2, 0.0, 1.0).astype(F32)
    zero_plane = jnp.zeros((X, Y), F32)

    def rows_of(ref, h0, n, x):
        return ref.reshape(H * X, Y)[pl.ds(h0 * X + x, n, stride=X), :]

    sx_p[0:16, :] = rows_of(r0, 0, 16, X - 1)
    sx_p[16:32, :] = rows_of(r0, 48, 16, X - 1)
    sx_p[32:40, :] = jnp.broadcast_to(opened[X - 1:X, :], (8, Y))
    sx_m[0:32, :] = rows_of(r0, 16, 32, 0)
    sx_m[32:40, :] = jnp.broadcast_to(opened[0:1, :], (8, Y))

    for k0, dst, shift in ((0, sy_p, 65), (2, sy_m, 64)):
        def pack(j, acc, k0=k0):
            return pack_column(acc, r0[k0 * 16 + j], j, k0)
        acc = lax.fori_loop(0, 32, pack, zero_plane, unroll=32)
        dst[...] = jnp.where(lane == 64, pltpu.roll(opened, shift, 1), acc)

    def value_row(i):
        return val.reshape(H * X, Y)[pl.ds(q * 8 + i, H, stride=X), :]

    def pack_values(rows, headings, side):
        acc = jnp.zeros((32, Y), F32)
        for i in range(8):
            part = rows[i][headings:headings + 32, :]
            shift = i + 1 if side else i
            acc = jnp.where(lane_h == i, pltpu.roll(part, shift, 1) if shift else part, acc)
        return acc

    low, high = q == 0, q == 3
    near_up = {"member": zh * 4 + jnp.where(low, y, (y + 4 - turn_sign) % 4), "gx": jnp.where(low, (gx + 7) % 8, gx)}
    near_down = {"member": zh * 4 + jnp.where(high, y, (y + turn_sign) % 4), "gx": jnp.where(high, (gx + 1) % 8, gx)}
    has_up, has_down = jnp.logical_or(q > 0, has_m), jnp.logical_or(q < 3, has_p)

    first = (
        (copy(ROW_DOWN, sx_p, hx_m, to_p), has_p, has_m),
        (copy(ROW_UP, sx_m, hx_p, to_m), has_m, has_p),
        (copy(COL_DOWN, sy_p, hy_m, to_e), east, west),
        (copy(COL_UP, sy_m, hy_p, to_w), west, east),
        (copy(VAL_DOWN, sv_p, hv_m, to_p), jnp.logical_and(high, has_p), jnp.logical_and(low, has_m)),
        (copy(VAL_UP, sv_m, hv_p, to_m), jnp.logical_and(low, has_m), jnp.logical_and(high, has_p)),
        (copy(VALCOL_DOWN, svc_p, hvc_m, to_e), east, west),
        (copy(VALCOL_UP, svc_m, hvc_p, to_w), west, east),
    )

    started, landed = [], set()

    def guarded(condition, act):
        if condition is True:
            act()
        else:
            pl.when(condition)(act)

    def launch(c, sends=True, receives=True):
        guarded(sends, c.start)
        started.append((c, sends, receives))
        return len(started) - 1

    def land(n):
        c, _, receives = started[n]
        guarded(receives, c.wait_recv)
        landed.add(n)

    def finish_all():
        for n, (c, sends, _) in enumerate(started):
            if n not in landed:
                land(n)
            guarded(sends, c.wait_send)

    pl.semaphore_wait(barrier, len(greeted) + has_m.astype(I32) + has_p.astype(I32))
    begun = [launch(*c) for c in first[:4]]
    @pl.when(gx == 0)
    def _():
        hx_m[...] = jnp.zeros((40, Y), F32)
        hv_m[...] = jnp.zeros((32, Y), F32)
        for k in (0, 3):
            h2x[k] = jnp.zeros((16, Y), F32)

    @pl.when(gx == 7)
    def _():
        hx_p[...] = jnp.zeros((40, Y), F32)
        hv_p[...] = jnp.zeros((32, Y), F32)
        for k in (1, 2):
            h2x[k] = jnp.zeros((16, Y), F32)

    @pl.when(gy == 0)
    def _():
        for ref in (hy_m, h2y.at[0], h2y.at[1], hvc_m, hc_m):
            ref[...] = zero_plane

    @pl.when(gy == 3)
    def _():
        for ref in (hy_p, h2y.at[2], h2y.at[3], hvc_p, hc_p):
            ref[...] = zero_plane

    @pl.when(jnp.logical_not(has_up))
    def _():
        hr_m[...] = jnp.zeros((32, Y), F32)

    @pl.when(jnp.logical_not(has_down))
    def _():
        hr_p[...] = jnp.zeros((32, Y), F32)

    loads[2].wait()
    own = [value_row(i) for i in range(8)]
    svc_p[...] = pack_values(own, 32, True)
    svc_m[...] = pack_values(own, 0, False)
    sv_p[...] = own[7][16:48, :]
    sv_m[0:16, :] = own[0][0:16, :]
    sv_m[16:32, :] = own[0][48:64, :]
    begun += [launch(*c) for c in first[4:]]
    for c in loads[3:]:
        c.wait()
    kf[:, 0:64] = kern[...]
    kf[:, 64:128] = kern[...]
    for n in begun[:4]:
        land(n)

    open_p = jnp.where(row == X - 1, hx_p[32:33, :], pltpu.roll(opened, X - 1, 0))
    open_m = jnp.where(row == 0, hx_m[32:33, :], pltpu.roll(opened, 1, 0))
    open_e = jnp.where(lane == Y - 1, pltpu.roll(hy_p[...], 63, 1), pltpu.roll(opened, Y - 1, 1))
    open_w = jnp.where(lane == 0, pltpu.roll(hy_m[...], 64, 1), pltpu.roll(opened, 1, 1))
    weights[0] = opened * open_p
    weights[1] = opened * open_m
    weights[2] = opened * open_e
    weights[3] = opened * open_w

    def transport(k, src, dst, halo_x, x_at, halo_y, y_at, packed):
        out_x, in_x = (0, 1) if k in (0, 3) else (1, 0)
        out_y, in_y = (2, 3) if k in (0, 1) else (3, 2)
        wox, wix, woy, wiy = weights[out_x], weights[in_x], weights[out_y], weights[in_y]
        kept = keep[...]
        columns = halo_y[...]
        h0 = 16 * k

        def turns(h):
            r = src[h]
            t = turn[h].astype(F32)
            up = jnp.maximum(t, 0.0) * r
            return r, up, up - t * r

        def start_of(j):
            h = h0 + j
            r, up, down = turns(h)
            ax = axt[pl.ds(h, 1), :]
            ay = ayt[pl.ds(h, 1), :]
            hx = halo_x[pl.ds(x_at + j, 1), :]
            xn = shift_x(r, hx, k)
            yn = shift_y(r, columns, y_at + j, k)
            s = r - up - down + ax * (wix * xn - wox * r) + ay * (wiy * yn - woy * r)
            return s, up, down

        _, up_before, _ = turns((h0 + 63) % 64)
        s, up, _ = start_of(0)
        carry = (s + up_before, up, zero_plane if packed is None else packed)

        def finish(j, partial, down, acc):
            new = (partial + down) * kept
            dst[h0 + j] = new
            return acc if packed is None else pack_column(acc, new, y_at + j, k)

        def body(j, carry):
            partial, up_last, acc = carry
            s, up, down = start_of(j)
            acc = finish(j - 1, partial, down, acc)
            return s + up_last, up, acc

        partial, _, acc = lax.fori_loop(1, 16, body, carry, unroll=15)
        _, _, down = turns((h0 + 16) % 64)
        return finish(15, partial, down, acc)

    def halos(k, row_m, row_p, column_m, column_p):
        return (
            ((row_m, 0), (row_p, 0), (row_p, 16), (row_m, 16))[k]
            + ((column_m, 0), (column_m, 16), (column_p, 0), (column_p, 16))[k]
        )

    second = []
    for k in range(4):
        s2y[k] = transport(k, r0, r1, *halos(k, hx_m, hx_p, hy_m, hy_p), zero_plane)
        s2x[k] = rows_of(r1, 16 * k, 16, X - 1 if k in (0, 3) else 0)
        target = (to_p, has_p, has_m) if k in (0, 3) else (to_m, has_m, has_p)
        second.append(launch(copy(STEP_ROW + k, s2x.at[k], h2x.at[k], target[0]), *target[1:]))
        target = (to_e, east, west) if k in (0, 1) else (to_w, west, east)
        second.append(launch(copy(STEP_COL + k, s2y.at[k], h2y.at[k], target[0]), *target[1:]))

    over_y = [[] for _ in range(CHUNKS)]
    for k in range(4):
        for n in second[2 * k:2 * k + 2]:
            land(n)
        transport(k, r1, r2, h2x.at[k], 0, h2y.at[k], (0, 16, 0, 16)[k], None)
        for c in range(k * CHUNKS // 4, (k + 1) * CHUNKS // 4):
            for d in (2, 1, 3):
                yy = (y + d) % 4
                qq = jnp.where(odd == 1, 3 - yy, yy)
                part = r2[pl.ds(CHUNK * c, CHUNK), pl.ds(pl.multiple_of(qq * 8, 8), 8), :]
                ysend[c, d - 1] = encode(part.reshape(ROWS, Y) * (1.0 / BOUND))
                there = copy(OVER_Y + 3 * c + d - 1, ysend.at[c, d - 1], yrecv.at[c, d - 1], at(zh, yy))
                over_y[c].append(launch(there))

    def count(z, yy):
        return counts[z * 4 + yy].astype(F32)

    def plane_of(scalar):
        return jnp.full((8, Y), scalar, F32)

    def group(z):
        return count(z, 0) + count(z, 1) + count(z, 2) + count(z, 3)

    mine, across = group(zh), [group(p) for p in pair]
    everyone = group(0) + group(1) + group(2) + group(3)
    inverse_all = 1.0 / plane_of(everyone)
    inverse_mine = (1.0 / BOUND) / plane_of(mine)

    def scaled(part, factor):
        return (part.reshape(CHUNK, 8, Y) * factor).reshape(ROWS, Y)

    over_z = [[None, None] for _ in range(CHUNKS)]
    for c in range(CHUNKS):
        block = pl.ds(CHUNK * c, CHUNK)
        part = r2[block, pl.ds(pl.multiple_of(q * 8, 8), 8), :].reshape(ROWS, Y) * count(zh, y)
        for n, d in zip(over_y[c], (2, 1, 3)):
            land(n)
            part = part + decode(yrecv[c, d - 1]) * count(zh, (y + 4 - d) % 4)
        zsend[c, 0] = encode(scaled(part, inverse_mine))
        over_z[c][0] = launch(copy(OVER_Z + 2 * c, zsend.at[c, 0], zrecv.at[c, 0], at(pair[c % 2], y)))

    for n in begun[4:]:
        land(n)

    @pl.when(low)
    def _():
        up_row[...] = hv_m[...]

    @pl.when(q > 0)
    def _():
        up_row[...] = val.reshape(H * X, Y)[pl.ds(16 * X + q * 8 - 1, 32, stride=X), :]

    @pl.when(high)
    def _():
        down_row[...] = hv_p[...]

    @pl.when(q < 3)
    def _():
        down_row[0:16, :] = val.reshape(H * X, Y)[pl.ds(q * 8 + 8, 16, stride=X), :]
        down_row[16:32, :] = val.reshape(H * X, Y)[pl.ds(48 * X + q * 8 + 8, 16, stride=X), :]

    wide_rows = pl.ds(pl.multiple_of(q * 8, 8), 8)
    w_rows = [weights[i, wide_rows, :] for i in range(4)]
    keep_rows = keep[wide_rows, :]
    kf_high, kf_low = split_left(kf[...])
    lane_c = lax.broadcasted_iota(I32, (64, 2 * Y), 1)
    kb = jnp.concatenate([kf_high, kf_low], axis=1)
    cf[:, 0:64] = coupling[...]
    cf[:, 64:128] = coupling[...]
    cf_high, cf_low = split_left(cf[...])
    cb = jnp.concatenate([cf_high, cf_low], axis=1)

    lane_of = lax.broadcasted_iota(I32, (32, Y), 1)

    def around(rows, before, after, first_column, last_column, i):
        v = rows[i]
        prior = rows[i - 1][16:48, :] if i > 0 else before
        if i < 7:
            later = (rows[i + 1][0:16, :], rows[i + 1][48:64, :])
        else:
            later = (after[0:16, :], after[16:32, :])
        north, south = pltpu.roll(v[0:32, :], Y - 1, 1), pltpu.roll(v[32:64, :], 1, 1)
        if last_column is not None:
            north = jnp.where(lane_of == Y - 1, pltpu.roll(last_column, Y - 1 - i, 1), north)
            south = jnp.where(lane_of == 0, pltpu.roll(first_column, Y - i, 1) if i else first_column, south)
        return v, prior, later, north, south, [w[i:i + 1, :] for w in w_rows]

    def reply(jobs):
        lowest_of, parts = [], []
        for v, prior, later, north, south, w in jobs:
            moves = []
            for k in range(4):
                part = slice(16 * k, 16 * k + 16)
                vk = v[part, :]
                xn = (later[0], prior[0:16, :], prior[16:32, :], later[1])[k]
                yn = (north[0:16, :], north[16:32, :], south[0:16, :], south[16:32, :])[k]
                wx = w[0 if k in (0, 3) else 1]
                wy = w[2 if k in (0, 1) else 3]
                moves.append(vk + axt[part, :] * (wx * (xn - vk)) + ayt[part, :] * (wy * (yn - vk)))
            moves = jnp.concatenate(moves, axis=0)
            lowest = jnp.min(moves, axis=0, keepdims=True)
            lowest_of.append(lowest)
            parts.append(jnp.exp((lowest - moves) * 10.0))
        summed = jnp.dot(cb, widen(jnp.concatenate(parts, axis=1)), preferred_element_type=F32)
        logs = jnp.log(summed) * 0.1
        return [lowest_of[n] - logs[:, n * Y:(n + 1) * Y] for n in range(len(jobs))]

    row_8 = lax.broadcasted_iota(I32, (8, Y), 0)
    lane_8 = lax.broadcasted_iota(I32, (8, Y), 1)

    def sides_of(w):
        first = jnp.where(lane_8 == row_8, w[:, 0:1], 0.0)
        last = jnp.where(lane_8 == row_8 + 8, w[:, Y - 1:Y], 0.0)
        return jnp.sum(first + last, axis=0, keepdims=True)

    w_sides = [sides_of(w) for w in w_rows]
    keep_sides = sides_of(keep_rows)

    def side_by_side(rows, first, last, part):
        acc = jnp.zeros((part.stop - part.start, Y), F32)
        lanes = lax.broadcasted_iota(I32, acc.shape, 1)
        for i in range(8):
            if first is not None:
                acc = jnp.where(lanes == i, pltpu.roll(rows[i][part, :], (i - first) % Y, 1), acc)
            if last is not None:
                acc = jnp.where(lanes == 8 + i, pltpu.roll(rows[i][part, :], (8 + i - last) % Y, 1), acc)
        return acc

    from_start = reply([around(own, up_row[...], down_row[...], hvc_m[...], hvc_p[...], i) for i in range(8)])
    for i in range(8):
        base[i] = from_start[i]

    lower = [jnp.full((8, Y), zh, I32) < jnp.full((8, Y), p, I32) for p in pair]

    def merge(c, stage, partner, weight_own, weight_other):
        a = decode(zsend[c, stage]).reshape(CHUNK, 8, Y) * weight_own
        b = decode(zrecv[c, stage]).reshape(CHUNK, 8, Y) * weight_other
        is_low = lower[partner]
        return jnp.where(is_low, a, b) + jnp.where(is_low, b, a)

    factors = [(1.0 / BOUND) / plane_of(mine + across[p]) for p in range(2)]
    for c in range(CHUNKS):
        p = c % 2
        land(over_z[c][0])
        both = merge(c, 0, p, mine, across[p])
        zsend[c, 1] = encode((both * factors[p]).reshape(ROWS, Y))
        over_z[c][1] = launch(copy(OVER_Z + 2 * c + 1, zsend.at[c, 1], zrecv.at[c, 1], at(pair[1 - p], y)))
    for c in range(CHUNKS):
        p = c % 2
        land(over_z[c][1])
        here = mine + across[p]
        mixed = merge(c, 1, 1 - p, here, everyone - here) * inverse_all
        total[pl.ds(ROWS * c, ROWS), :] = mixed.reshape(ROWS, Y)

    mixed_rows = jnp.concatenate([total[pl.ds(i, H, stride=8), :] for i in range(8)], axis=1)
    running = 0.5 + 0.5 * jnp.dot(kb, widen(mixed_rows), preferred_element_type=F32)
    cost = [running[:, i * Y:(i + 1) * Y] for i in range(8)]
    once = [(cost[i] + base[i]) * keep_rows[i:i + 1, :] for i in range(8)]

    sr_p[...] = once[7][16:48, :]
    sr_m[0:16, :] = once[0][0:16, :]
    sr_m[16:32, :] = once[0][48:64, :]
    sc_p[...] = pack_values(once, 32, True)
    sc_m[...] = pack_values(once, 0, False)
    edges = (
        (copy(REPLY, sr_p, hr_m, near_down), has_down, has_up),
        (copy(REPLY + 1, sr_m, hr_p, near_up), has_up, has_down),
        (copy(REPLY + 2, sc_p, hc_m, to_e), east, west),
        (copy(REPLY + 3, sc_m, hc_p, to_w), west, east),
    )
    edges = [launch(*c) for c in edges]

    def code_of(v, eighths):
        inverse = (32767.0 * 8.0) / eighths.astype(F32)
        return ((v * inverse + 32768.5).astype(I32) - 32768).astype(I16)

    def eighths_of(v):
        return (jnp.max(jnp.abs(v), axis=0, keepdims=True) * 8.0).astype(I32) + 1

    def send_piece(piece, rows, tile):
        for n in range(SPAN):
            gsend[piece, pl.ds(H * n, H), :] = rows[n]
        gsend[piece, pl.ds(MARK, 16), :] = tile
        out = []
        for d in (2, 1, 3):
            there = copy(GATHER + 3 * piece + d - 1, gsend.at[piece], grecv.at[piece, d - 1], at(zh, (y + d) % 4))
            out.append((launch(there), piece, d))
        return out

    def closed(i, t):
        return (cost[i] + t) * keep_rows[i:i + 1, :]

    gathers = []
    for piece in range(PIECES - 1):
        indices = (2 * piece + 1, 2 * piece + 2)
        twice = [closed(i, t) for i, t in zip(indices, reply([around(once, None, None, None, None, i) for i in indices]))]
        eighths = eighths_of(jnp.concatenate(twice, axis=0))
        tile = jnp.broadcast_to(eighths, (16, Y)).astype(I16)
        gathers += send_piece(piece, [code_of(v, eighths) for v in twice], tile)
    whole = slice(0, H)
    sides = side_by_side(once, 0, Y - 1, whole)
    cost_sides = side_by_side(cost, 0, Y - 1, whole)
    inner_first = side_by_side(once, 1, None, slice(0, 32))
    inner_last = side_by_side(once, None, Y - 2, slice(32, H))
    after_sides, before_sides = pltpu.roll(sides, Y - 1, 1), pltpu.roll(sides, 1, 1)
    for n in edges:
        land(n)
    last_three = reply((
        around(once, hr_m[...], hr_p[...], hc_m[...], hc_p[...], 0),
        around(once, hr_m[...], hr_p[...], hc_m[...], hc_p[...], 7),
        (
            sides, before_sides[16:48, :], (after_sides[0:16, :], after_sides[48:64, :]),
            jnp.where(lane_of < 8, inner_first, pltpu.roll(hc_p[...], 8, 1)),
            jnp.where(lane_of < 8, hc_m[...], inner_last), w_sides,
        ),
    ))
    ends = (closed(0, last_three[0]), closed(7, last_three[1]))
    columns = (cost_sides + last_three[2]) * keep_sides
    patch = columns[0:8, :]
    for n in range(1, 8):
        here = jnp.logical_and(lane_8 >= 16 * n, lane_8 < 16 * n + 16)
        patch = jnp.where(here, pltpu.roll(columns[8 * n:8 * n + 8, :], 16 * n, 1), patch)
    eighths = eighths_of(jnp.concatenate(ends, axis=0))
    eighths_patch = eighths_of(patch)
    scales = jnp.where(row_8 < 4, eighths, eighths_patch)
    inverse = (32767.0 * 8.0) / eighths_patch.astype(F32)
    patch_code = (patch * inverse + 32768.5).astype(I32) - 32768
    tile = jnp.concatenate([scales, patch_code], axis=0).astype(I16)
    gathers += send_piece(PIECES - 1, [code_of(v, eighths) for v in ends], tile)

    lane_w = lax.broadcasted_iota(I32, (H, Y), 1)
    out_rows = out.reshape(H * X, Y)

    def unpack(codes, qq, piece):
        scale = codes[MARK:MARK + 1, :].astype(F32) * (0.125 / 32767.0)
        indices = (2 * piece + 1, 2 * piece + 2) if piece < PIECES - 1 else (0, 7)
        for n, i in enumerate(indices):
            out_rows[pl.ds(qq * 8 + i, H, stride=X), :] = codes[H * n:H * n + H, :].astype(F32) * scale
        if piece < PIECES - 1:
            return
        scale = codes[MARK + 4:MARK + 5, :].astype(F32) * (0.125 / 32767.0)
        flat = codes[MARK + 8:MARK + 16, :].astype(F32) * scale
        wide = jnp.concatenate([pltpu.roll(flat, Y - 16 * n, 1) if n else flat for n in range(8)], axis=0)
        for i in range(1, 7):
            at_row = pl.ds(qq * 8 + i, H, stride=X)
            v = jnp.where(lane_w == 0, pltpu.roll(wide, Y - i, 1), out_rows[at_row, :])
            out_rows[at_row, :] = jnp.where(lane_w == Y - 1, pltpu.roll(wide, Y - 9 - i, 1), v)

    for piece in range(PIECES):
        unpack(gsend[piece].astype(I32), q, piece)
    for n, piece, d in gathers:
        land(n)
        yy = (y + 4 - d) % 4
        unpack(grecv[piece, d - 1].astype(I32), jnp.where(odd == 1, 3 - yy, yy), piece)
    finish_all()


def write_out(moved, values, moved_out, values_out, sems):
    copies = [
        pltpu.make_async_copy(src, dst, sems.at[i])
        for i, (src, dst) in enumerate(((moved, moved_out), (values, values_out)))
    ]
    for c in copies:
        c.start()
    for c in copies:
        c.wait()


def shards(density, turn_rate, value_init, labels, counts, kernel_matrix):
    along_x, along_y, coupling = tables()
    vmem = lambda *shape: pltpu.VMEM(shape, F32)
    in_hbm = pl.BlockSpec(memory_space=pltpu.HBM)
    scratch = [
        vmem(H, X, Y), pltpu.VMEM((H, X, Y), BF16), vmem(H, X, Y), pltpu.VMEM((X, Y), I32), vmem(H, Y), vmem(H, Y),
        vmem(H, H), vmem(H, H),
        vmem(40, Y), vmem(40, Y), *[vmem(32, Y) for _ in range(6)],
        vmem(40, Y), vmem(40, Y), *[vmem(32, Y) for _ in range(6)],
        vmem(H, X, Y), vmem(4, 16, Y), vmem(4, X, Y), vmem(4, 16, Y), vmem(4, X, Y), vmem(4, X, Y),
        vmem(X, Y),
        pltpu.VMEM((CHUNKS, 3, ROWS, Y), I16), pltpu.VMEM((CHUNKS, 3, ROWS, Y), I16),
        pltpu.VMEM((CHUNKS, 2, ROWS, Y), I16), pltpu.VMEM((CHUNKS, 2, ROWS, Y), I16), vmem(512, Y), vmem(8, H, Y),
        vmem(32, Y), vmem(32, Y), vmem(8, Y), vmem(H, 128), vmem(H, 128),
        *[vmem(32, Y) for _ in range(8)],
        pltpu.VMEM((PIECES, MARK + 16, Y), I16), pltpu.VMEM((PIECES, 3, MARK + 16, Y), I16),
        pltpu.SMEM((16,), I32), pltpu.SemaphoreType.DMA((9,)),
        pltpu.SemaphoreType.DMA((COPIES,)), pltpu.SemaphoreType.DMA((COPIES,)),
    ]
    held = pltpu.VMEM((H, X, Y), F32)
    in_vmem = pl.BlockSpec(memory_space=pltpu.VMEM)
    operands = (
        counts, density[0], turn_rate[0], value_init, labels,
        jnp.asarray(along_x), jnp.asarray(along_y), jnp.asarray(coupling), kernel_matrix,
    )
    moved, values = pl.pallas_call(
        kernel,
        out_shape=(held, held),
        in_specs=[in_hbm] * 9,
        out_specs=(in_vmem, in_vmem),
        scratch_shapes=scratch,
        compiler_params=pltpu.CompilerParams(
            collective_id=1, has_side_effects=True, vmem_limit_bytes=40 * 1024 * 1024
        ),
        name="play",
    )(*[pltpu.with_memory_space_constraint(a, pltpu.HBM) for a in operands])
    whole = jax.ShapeDtypeStruct((H, X, Y), F32)
    moved, values = pl.pallas_call(
        write_out,
        out_shape=(whole, whole),
        in_specs=[in_vmem, in_vmem],
        out_specs=(in_hbm, in_hbm),
        scratch_shapes=[pltpu.SemaphoreType.DMA((2,))],
        compiler_params=pltpu.CompilerParams(vmem_limit_bytes=8 * 1024 * 1024),
        name="write",
    )(moved, values)
    return moved[None], values


def solution(mesh):
    placed = (
        P("member", None, "gx", "gy"),
        P("member", None, "gx", "gy"),
        P(None, "gx", "gy"),
        P("gx", "gy"),
        P(),
        P(),
    )
    return jax.shard_map(
        shards,
        mesh=mesh,
        in_specs=placed,
        out_specs=(P("member", None, "gx", "gy"), P(None, "gx", "gy")),
        check_vma=False,
    )
```

```python
import jax
import jax.numpy as jnp
import numpy as np
from jax import lax
from jax.experimental import pallas as pl
from jax.experimental.pallas import tpu as pltpu
from jax.sharding import PartitionSpec as P

MESH = pl.DeviceIdType.MESH
F32 = jnp.float32
BF16 = jnp.bfloat16
I16 = jnp.int16
I32 = jnp.int32

H, X, Y = 64, 32, 128
SPEED = 0.55
BOUND = 9.5

ROW_UP, ROW_DOWN, COL_UP, COL_DOWN, VAL_UP, VAL_DOWN, VALCOL_UP, VALCOL_DOWN = range(8)
CHUNK = 8
CHUNKS = H // CHUNK
ROWS = 8 * CHUNK
STEP_ROW, STEP_COL, OVER_Y = 8, 12, 16
OVER_Z = OVER_Y + 3 * CHUNKS
REPLY = OVER_Z + 2 * CHUNKS
GATHER = REPLY + 4
PIECES = 4
SPAN = 8 // PIECES
MARK = H * SPAN
COPIES = GATHER + 3 * PIECES


def tables():
    angles = np.arange(H, dtype=np.float32) * np.float32(2.0 * np.pi / H)
    along_x = np.abs(SPEED * np.cos(angles)).astype(np.float32)
    along_y = np.abs(SPEED * np.sin(angles)).astype(np.float32)
    spread = angles[:, None] - angles[None, :]
    coupling = np.exp(-5.0 * (1.0 - np.cos(spread.astype(np.float64)))).astype(np.float32)
    wide = lambda v: np.ascontiguousarray(np.broadcast_to(v[:, None], (H, Y)))
    return wide(along_x), wide(along_y), coupling


def encode(x):
    root = jnp.sqrt(jnp.maximum(x, 0.0)) * 65535.0 + 0.5
    return (root.astype(I32) - 32768).astype(I16)


def decode(code):
    root = code.astype(I32).astype(F32) + 32768.0
    return root * root * (BOUND / (65535.0 * 65535.0))


def split_left(m):
    high = m.astype(BF16)
    low = (m - high.astype(F32)).astype(BF16)
    return high, low


def widen(m):
    high, low = split_left(m)
    return jnp.concatenate([high, low, high, low], axis=0)


def kernel(
    counts_hbm, density, turn_hbm, value_hbm, labels_hbm, ax_hbm, ay_hbm, coupling_hbm, kernel_hbm,
    r2, out,
    r0, turn, val, labels, axt, ayt, coupling, kern,
    sx_m, sx_p, sy_m, sy_p, sv_m, sv_p, svc_m, svc_p, hx_m, hx_p, hy_m, hy_p, hv_m, hv_p, hvc_m, hvc_p,
    r1, s2x, s2y, h2x, h2y, weights, keep,
    ysend, yrecv, zsend, zrecv, total, base,
    up_row, down_row, cs, kf, cf,
    sr_m, sr_p, sc_m, sc_p, hr_m, hr_p, hc_m, hc_p,
    gsend, grecv,
    counts, word, load_sem, ss, rs,
):
    member = lax.axis_index("member")
    gx = lax.axis_index("gx")
    gy = lax.axis_index("gy")
    zh, y = member // 4, member % 4
    odd = gx % 2
    q = jnp.where(odd == 1, 3 - y, y)
    turn_sign = jnp.where(odd == 1, 3, 1)

    def at(z, yy):
        return {"member": z * 4 + yy}

    pair = (jnp.where(zh % 2 == 0, zh + 1, zh - 1), 3 - zh)

    quads = [pl.ds(16 * k, 16) for k in (0, 3, 1, 2)]
    loads = [
        pltpu.make_async_copy(src, dst, load_sem.at[i])
        for i, (src, dst) in enumerate((
            *[(density.at[b], r0.at[b]) for b in quads],
            (labels_hbm, labels), (turn_hbm, turn), (value_hbm, val), (ax_hbm, axt), (ay_hbm, ayt),
            (coupling_hbm, coupling), (kernel_hbm, kern), (counts_hbm, counts),
        ))
    ]
    for c in loads[:5]:
        c.start()

    barrier = pltpu.get_barrier_semaphore()
    z_lo, core = gx // 2, gx % 2
    z_up, z_down = (zh * 4 + z_lo + 1) % 16, (zh * 4 + z_lo + 15) % 16
    beside = [{"member": (z // 4) * 4 + y, "gx": (z % 4) * 2 + core} for z in (z_up, z_down)]
    greeted = [at(zh, (y + d) % 4) for d in (1, 2, 3)] + beside
    greeted += [{"gy": (gy + d) % 4} for d in (1, 3)]

    def greet(target):
        pl.semaphore_signal(barrier, inc=1, device_id=target, device_id_type=MESH)

    has_m, has_p = gx > 0, gx < 7
    west, east = gy > 0, gy < 3
    to_m, to_p = {"gx": (gx + 7) % 8}, {"gx": (gx + 1) % 8}
    to_w, to_e = {"gy": (gy + 3) % 4}, {"gy": (gy + 1) % 4}
    pl.when(has_m)(lambda: greet(to_m))
    pl.when(has_p)(lambda: greet(to_p))
    for target in greeted:
        greet(target)

    for c in loads[5:]:
        c.start()

    def copy(i, src, dst, target):
        return pltpu.make_async_remote_copy(
            src_ref=src, dst_ref=dst, send_sem=ss.at[i], recv_sem=rs.at[i], device_id=target, device_id_type=MESH
        )

    lane = lax.broadcasted_iota(I32, (X, Y), 1)
    row = lax.broadcasted_iota(I32, (X, Y), 0)
    lane_h = lax.broadcasted_iota(I32, (32, Y), 1)

    def shift_x(r, halo, k):
        if k in (0, 3):
            return jnp.where(row == 0, halo, pltpu.roll(r, 1, 0))
        return jnp.where(row == X - 1, halo, pltpu.roll(r, X - 1, 0))

    def shift_y(r, halo, position, k):
        if k in (0, 1):
            moved_halo = pltpu.roll(halo, lax.rem(Y - position, Y), 1)
            return jnp.where(lane == 0, moved_halo, pltpu.roll(r, 1, 1))
        moved_halo = pltpu.roll(halo, Y - 1 - position, 1)
        return jnp.where(lane == Y - 1, moved_halo, pltpu.roll(r, Y - 1, 1))

    def pack_column(acc, r, position, k):
        shift = position + 1 if k in (0, 1) else position
        return jnp.where(lane == position, pltpu.roll(r, shift, 1), acc)

    for c in loads[:5]:
        c.wait()
    opened = jnp.where(labels[...] != 1, 1.0, 0.0).astype(F32)
    keep[...] = jnp.where(labels[...] == 2, 0.0, 1.0).astype(F32)
    zero_plane = jnp.zeros((X, Y), F32)

    def rows_of(ref, h0, n, x):
        return ref.reshape(H * X, Y)[pl.ds(h0 * X + x, n, stride=X), :]

    sx_p[0:16, :] = rows_of(r0, 0, 16, X - 1)
    sx_p[16:32, :] = rows_of(r0, 48, 16, X - 1)
    sx_p[32:40, :] = jnp.broadcast_to(opened[X - 1:X, :], (8, Y))
    sx_m[0:32, :] = rows_of(r0, 16, 32, 0)
    sx_m[32:40, :] = jnp.broadcast_to(opened[0:1, :], (8, Y))

    for k0, dst, shift in ((0, sy_p, 65), (2, sy_m, 64)):
        def pack(j, acc, k0=k0):
            return pack_column(acc, r0[k0 * 16 + j], j, k0)
        acc = lax.fori_loop(0, 32, pack, zero_plane, unroll=32)
        dst[...] = jnp.where(lane == 64, pltpu.roll(opened, shift, 1), acc)

    def value_row(i):
        return val.reshape(H * X, Y)[pl.ds(q * 8 + i, H, stride=X), :]

    def pack_values(rows, headings, side):
        acc = jnp.zeros((32, Y), F32)
        for i in range(8):
            part = rows[i][headings:headings + 32, :]
            shift = i + 1 if side else i
            acc = jnp.where(lane_h == i, pltpu.roll(part, shift, 1) if shift else part, acc)
        return acc

    low, high = q == 0, q == 3
    near_up = {"member": zh * 4 + jnp.where(low, y, (y + 4 - turn_sign) % 4), "gx": jnp.where(low, (gx + 7) % 8, gx)}
    near_down = {"member": zh * 4 + jnp.where(high, y, (y + turn_sign) % 4), "gx": jnp.where(high, (gx + 1) % 8, gx)}
    has_up, has_down = jnp.logical_or(q > 0, has_m), jnp.logical_or(q < 3, has_p)

    first = (
        (copy(ROW_DOWN, sx_p, hx_m, to_p), has_p, has_m),
        (copy(ROW_UP, sx_m, hx_p, to_m), has_m, has_p),
        (copy(COL_DOWN, sy_p, hy_m, to_e), east, west),
        (copy(COL_UP, sy_m, hy_p, to_w), west, east),
        (copy(VAL_DOWN, sv_p, hv_m, to_p), jnp.logical_and(high, has_p), jnp.logical_and(low, has_m)),
        (copy(VAL_UP, sv_m, hv_p, to_m), jnp.logical_and(low, has_m), jnp.logical_and(high, has_p)),
        (copy(VALCOL_DOWN, svc_p, hvc_m, to_e), east, west),
        (copy(VALCOL_UP, svc_m, hvc_p, to_w), west, east),
    )

    started, landed = [], set()

    def guarded(condition, act):
        if condition is True:
            act()
        else:
            pl.when(condition)(act)

    def launch(c, sends=True, receives=True):
        guarded(sends, c.start)
        started.append((c, sends, receives))
        return len(started) - 1

    def land(n):
        c, _, receives = started[n]
        guarded(receives, c.wait_recv)
        landed.add(n)

    sent = set()

    def settle(upto):
        for n in range(upto):
            if n not in sent:
                c, sends, _ = started[n]
                guarded(sends, c.wait_send)
                sent.add(n)

    def finish_all():
        for n in range(len(started)):
            if n not in landed:
                land(n)
        settle(len(started))

    pl.semaphore_wait(barrier, len(greeted) + has_m.astype(I32) + has_p.astype(I32))

    def pass_word(n):
        for target in beside:
            pl.semaphore_signal(word.at[n], inc=1, device_id=target, device_id_type=MESH)

    pass_word(0)
    begun = [launch(*c) for c in first[:4]]
    @pl.when(gx == 0)
    def _():
        hx_m[...] = jnp.zeros((40, Y), F32)
        hv_m[...] = jnp.zeros((32, Y), F32)
        for k in (0, 3):
            h2x[k] = jnp.zeros((16, Y), F32)

    @pl.when(gx == 7)
    def _():
        hx_p[...] = jnp.zeros((40, Y), F32)
        hv_p[...] = jnp.zeros((32, Y), F32)
        for k in (1, 2):
            h2x[k] = jnp.zeros((16, Y), F32)

    @pl.when(gy == 0)
    def _():
        for ref in (hy_m, h2y.at[0], h2y.at[1], hvc_m, hc_m):
            ref[...] = zero_plane

    @pl.when(gy == 3)
    def _():
        for ref in (hy_p, h2y.at[2], h2y.at[3], hvc_p, hc_p):
            ref[...] = zero_plane

    @pl.when(jnp.logical_not(has_up))
    def _():
        hr_m[...] = jnp.zeros((32, Y), F32)

    @pl.when(jnp.logical_not(has_down))
    def _():
        hr_p[...] = jnp.zeros((32, Y), F32)

    loads[6].wait()
    own = [value_row(i) for i in range(8)]
    svc_p[...] = pack_values(own, 32, True)
    svc_m[...] = pack_values(own, 0, False)
    sv_p[...] = own[7][16:48, :]
    sv_m[0:16, :] = own[0][0:16, :]
    sv_m[16:32, :] = own[0][48:64, :]
    begun += [launch(*c) for c in first[4:]]
    for n in (5, 7, 8, 9, 10, 11):
        loads[n].wait()
    kf[:, 0:64] = kern[...]
    kf[:, 64:128] = kern[...]
    for n in begun[:4]:
        land(n)

    open_p = jnp.where(row == X - 1, hx_p[32:33, :], pltpu.roll(opened, X - 1, 0))
    open_m = jnp.where(row == 0, hx_m[32:33, :], pltpu.roll(opened, 1, 0))
    open_e = jnp.where(lane == Y - 1, pltpu.roll(hy_p[...], 63, 1), pltpu.roll(opened, Y - 1, 1))
    open_w = jnp.where(lane == 0, pltpu.roll(hy_m[...], 64, 1), pltpu.roll(opened, 1, 1))
    weights[0] = opened * open_p
    weights[1] = opened * open_m
    weights[2] = opened * open_e
    weights[3] = opened * open_w

    def transport(k, src, dst, halo_x, x_at, halo_y, y_at, packed):
        out_x, in_x = (0, 1) if k in (0, 3) else (1, 0)
        out_y, in_y = (2, 3) if k in (0, 1) else (3, 2)
        wox, wix, woy, wiy = weights[out_x], weights[in_x], weights[out_y], weights[in_y]
        kept = keep[...]
        columns = halo_y[...]
        h0 = 16 * k

        def turns(h):
            r = src[h]
            t = turn[h].astype(F32)
            up = jnp.maximum(t, 0.0) * r
            return r, up, up - t * r

        def start_of(j):
            h = h0 + j
            r, up, down = turns(h)
            ax = axt[pl.ds(h, 1), :]
            ay = ayt[pl.ds(h, 1), :]
            hx = halo_x[pl.ds(x_at + j, 1), :]
            xn = shift_x(r, hx, k)
            yn = shift_y(r, columns, y_at + j, k)
            s = r - up - down + ax * (wix * xn - wox * r) + ay * (wiy * yn - woy * r)
            return s, up, down

        _, up_before, _ = turns((h0 + 63) % 64)
        s, up, _ = start_of(0)
        carry = (s + up_before, up, zero_plane if packed is None else packed)

        def finish(j, partial, down, acc):
            new = (partial + down) * kept
            dst[h0 + j] = new
            return acc if packed is None else pack_column(acc, new, y_at + j, k)

        def body(j, carry):
            partial, up_last, acc = carry
            s, up, down = start_of(j)
            acc = finish(j - 1, partial, down, acc)
            return s + up_last, up, acc

        partial, _, acc = lax.fori_loop(1, 16, body, carry, unroll=15)
        _, _, down = turns((h0 + 16) % 64)
        return finish(15, partial, down, acc)

    def halos(k, row_m, row_p, column_m, column_p):
        return (
            ((row_m, 0), (row_p, 0), (row_p, 16), (row_m, 16))[k]
            + ((column_m, 0), (column_m, 16), (column_p, 0), (column_p, 16))[k]
        )

    second = []
    for k in range(4):
        s2y[k] = transport(k, r0, r1, *halos(k, hx_m, hx_p, hy_m, hy_p), zero_plane)
        s2x[k] = rows_of(r1, 16 * k, 16, X - 1 if k in (0, 3) else 0)
        target = (to_p, has_p, has_m) if k in (0, 3) else (to_m, has_m, has_p)
        second.append(launch(copy(STEP_ROW + k, s2x.at[k], h2x.at[k], target[0]), *target[1:]))
        target = (to_e, east, west) if k in (0, 1) else (to_w, west, east)
        second.append(launch(copy(STEP_COL + k, s2y.at[k], h2y.at[k], target[0]), *target[1:]))

    pl.semaphore_wait(word.at[0], 2)
    pass_word(1)

    over_y = [[] for _ in range(CHUNKS)]
    for k in range(4):
        for n in second[2 * k:2 * k + 2]:
            land(n)
        transport(k, r1, r2, h2x.at[k], 0, h2y.at[k], (0, 16, 0, 16)[k], None)
        for c in range(k * CHUNKS // 4, (k + 1) * CHUNKS // 4):
            for d in (2, 1, 3):
                yy = (y + d) % 4
                qq = jnp.where(odd == 1, 3 - yy, yy)
                part = r2[pl.ds(CHUNK * c, CHUNK), pl.ds(pl.multiple_of(qq * 8, 8), 8), :]
                ysend[c, d - 1] = encode(part.reshape(ROWS, Y) * (1.0 / BOUND))
                there = copy(OVER_Y + 3 * c + d - 1, ysend.at[c, d - 1], yrecv.at[c, d - 1], at(zh, yy))
                over_y[c].append(launch(there))
    pl.semaphore_wait(word.at[1], 2)
    pass_word(2)

    def count(z, yy):
        return counts[z * 4 + yy].astype(F32)

    def plane_of(scalar):
        return jnp.full((8, Y), scalar, F32)

    def group(z):
        return count(z, 0) + count(z, 1) + count(z, 2) + count(z, 3)

    mine, across = group(zh), [group(p) for p in pair]
    everyone = group(0) + group(1) + group(2) + group(3)
    inverse_all = 1.0 / plane_of(everyone)
    inverse_mine = (1.0 / BOUND) / plane_of(mine)

    def scaled(part, factor):
        return (part.reshape(CHUNK, 8, Y) * factor).reshape(ROWS, Y)

    pl.semaphore_wait(word.at[2], 2)
    over_z = [[None, None] for _ in range(CHUNKS)]
    for c in range(CHUNKS):
        block = pl.ds(CHUNK * c, CHUNK)
        part = r2[block, pl.ds(pl.multiple_of(q * 8, 8), 8), :].reshape(ROWS, Y) * count(zh, y)
        for n, d in zip(over_y[c], (2, 1, 3)):
            land(n)
            part = part + decode(yrecv[c, d - 1]) * count(zh, (y + 4 - d) % 4)
        zsend[c, 0] = encode(scaled(part, inverse_mine))
        over_z[c][0] = launch(copy(OVER_Z + 2 * c, zsend.at[c, 0], zrecv.at[c, 0], at(pair[c % 2], y)))

    for n in begun[4:]:
        land(n)

    @pl.when(low)
    def _():
        up_row[...] = hv_m[...]

    @pl.when(q > 0)
    def _():
        up_row[...] = val.reshape(H * X, Y)[pl.ds(16 * X + q * 8 - 1, 32, stride=X), :]

    @pl.when(high)
    def _():
        down_row[...] = hv_p[...]

    @pl.when(q < 3)
    def _():
        down_row[0:16, :] = val.reshape(H * X, Y)[pl.ds(q * 8 + 8, 16, stride=X), :]
        down_row[16:32, :] = val.reshape(H * X, Y)[pl.ds(48 * X + q * 8 + 8, 16, stride=X), :]

    wide_rows = pl.ds(pl.multiple_of(q * 8, 8), 8)
    w_rows = [weights[i, wide_rows, :] for i in range(4)]
    keep_rows = keep[wide_rows, :]
    kf_high, kf_low = split_left(kf[...])
    lane_c = lax.broadcasted_iota(I32, (64, 2 * Y), 1)
    kb = jnp.concatenate([kf_high, kf_low], axis=1)
    cf[:, 0:64] = coupling[...]
    cf[:, 64:128] = coupling[...]
    cf_high, cf_low = split_left(cf[...])
    cb = jnp.concatenate([cf_high, cf_low], axis=1)

    lane_of = lax.broadcasted_iota(I32, (32, Y), 1)

    def around(rows, before, after, first_column, last_column, i):
        v = rows[i]
        prior = rows[i - 1][16:48, :] if i > 0 else before
        if i < 7:
            later = (rows[i + 1][0:16, :], rows[i + 1][48:64, :])
        else:
            later = (after[0:16, :], after[16:32, :])
        north, south = pltpu.roll(v[0:32, :], Y - 1, 1), pltpu.roll(v[32:64, :], 1, 1)
        if last_column is not None:
            north = jnp.where(lane_of == Y - 1, pltpu.roll(last_column, Y - 1 - i, 1), north)
            south = jnp.where(lane_of == 0, pltpu.roll(first_column, Y - i, 1) if i else first_column, south)
        return v, prior, later, north, south, [w[i:i + 1, :] for w in w_rows]

    def reply(jobs):
        lowest_of, parts = [], []
        for v, prior, later, north, south, w in jobs:
            moves = []
            for k in range(4):
                part = slice(16 * k, 16 * k + 16)
                vk = v[part, :]
                xn = (later[0], prior[0:16, :], prior[16:32, :], later[1])[k]
                yn = (north[0:16, :], north[16:32, :], south[0:16, :], south[16:32, :])[k]
                wx = w[0 if k in (0, 3) else 1]
                wy = w[2 if k in (0, 1) else 3]
                moves.append(vk + axt[part, :] * (wx * (xn - vk)) + ayt[part, :] * (wy * (yn - vk)))
            moves = jnp.concatenate(moves, axis=0)
            lowest = jnp.min(moves, axis=0, keepdims=True)
            lowest_of.append(lowest)
            parts.append(jnp.exp((lowest - moves) * 10.0))
        summed = jnp.dot(cb, widen(jnp.concatenate(parts, axis=1)), preferred_element_type=F32)
        logs = jnp.log(summed) * 0.1
        return [lowest_of[n] - logs[:, n * Y:(n + 1) * Y] for n in range(len(jobs))]

    row_8 = lax.broadcasted_iota(I32, (8, Y), 0)
    lane_8 = lax.broadcasted_iota(I32, (8, Y), 1)

    def sides_of(w):
        first = jnp.where(lane_8 == row_8, w[:, 0:1], 0.0)
        last = jnp.where(lane_8 == row_8 + 8, w[:, Y - 1:Y], 0.0)
        return jnp.sum(first + last, axis=0, keepdims=True)

    w_sides = [sides_of(w) for w in w_rows]
    keep_sides = sides_of(keep_rows)

    def side_by_side(rows, first, last, part):
        acc = jnp.zeros((part.stop - part.start, Y), F32)
        lanes = lax.broadcasted_iota(I32, acc.shape, 1)
        for i in range(8):
            if first is not None:
                acc = jnp.where(lanes == i, pltpu.roll(rows[i][part, :], (i - first) % Y, 1), acc)
            if last is not None:
                acc = jnp.where(lanes == 8 + i, pltpu.roll(rows[i][part, :], (8 + i - last) % Y, 1), acc)
        return acc

    from_start = reply([around(own, up_row[...], down_row[...], hvc_m[...], hvc_p[...], i) for i in range(8)])
    for i in range(8):
        base[i] = from_start[i]

    lower = [jnp.full((8, Y), zh, I32) < jnp.full((8, Y), p, I32) for p in pair]

    def merge(c, stage, partner, weight_own, weight_other):
        a = decode(zsend[c, stage]).reshape(CHUNK, 8, Y) * weight_own
        b = decode(zrecv[c, stage]).reshape(CHUNK, 8, Y) * weight_other
        is_low = lower[partner]
        return jnp.where(is_low, a, b) + jnp.where(is_low, b, a)

    factors = [(1.0 / BOUND) / plane_of(mine + across[p]) for p in range(2)]
    for c in range(CHUNKS):
        p = c % 2
        land(over_z[c][0])
        both = merge(c, 0, p, mine, across[p])
        zsend[c, 1] = encode((both * factors[p]).reshape(ROWS, Y))
        over_z[c][1] = launch(copy(OVER_Z + 2 * c + 1, zsend.at[c, 1], zrecv.at[c, 1], at(pair[1 - p], y)))
    for c in range(CHUNKS):
        p = c % 2
        land(over_z[c][1])
        here = mine + across[p]
        mixed = merge(c, 1, 1 - p, here, everyone - here) * inverse_all
        total[pl.ds(ROWS * c, ROWS), :] = mixed.reshape(ROWS, Y)

    mixed_rows = jnp.concatenate([total[pl.ds(i, H, stride=8), :] for i in range(8)], axis=1)
    running = 0.5 + 0.5 * jnp.dot(kb, widen(mixed_rows), preferred_element_type=F32)
    cost = [running[:, i * Y:(i + 1) * Y] for i in range(8)]
    once = [(cost[i] + base[i]) * keep_rows[i:i + 1, :] for i in range(8)]

    sr_p[...] = once[7][16:48, :]
    sr_m[0:16, :] = once[0][0:16, :]
    sr_m[16:32, :] = once[0][48:64, :]
    sc_p[...] = pack_values(once, 32, True)
    sc_m[...] = pack_values(once, 0, False)
    edges = (
        (copy(REPLY, sr_p, hr_m, near_down), has_down, has_up),
        (copy(REPLY + 1, sr_m, hr_p, near_up), has_up, has_down),
        (copy(REPLY + 2, sc_p, hc_m, to_e), east, west),
        (copy(REPLY + 3, sc_m, hc_p, to_w), west, east),
    )
    before_edges = len(started)
    edges = [launch(*c) for c in edges]

    def code_of(v, eighths):
        inverse = (32767.0 * 8.0) / eighths.astype(F32)
        return ((v * inverse + 32768.5).astype(I32) - 32768).astype(I16)

    def eighths_of(v):
        return (jnp.max(jnp.abs(v), axis=0, keepdims=True) * 8.0).astype(I32) + 1

    def send_piece(piece, rows, tile):
        for n in range(SPAN):
            gsend[piece, pl.ds(H * n, H), :] = rows[n]
        gsend[piece, pl.ds(MARK, 16), :] = tile
        out = []
        for d in (2, 1, 3):
            there = copy(GATHER + 3 * piece + d - 1, gsend.at[piece], grecv.at[piece, d - 1], at(zh, (y + d) % 4))
            out.append((launch(there), piece, d))
        return out

    def closed(i, t):
        return (cost[i] + t) * keep_rows[i:i + 1, :]

    gathers = []
    for piece in range(PIECES - 1):
        indices = (2 * piece + 1, 2 * piece + 2)
        twice = [closed(i, t) for i, t in zip(indices, reply([around(once, None, None, None, None, i) for i in indices]))]
        eighths = eighths_of(jnp.concatenate(twice, axis=0))
        tile = jnp.broadcast_to(eighths, (16, Y)).astype(I16)
        gathers += send_piece(piece, [code_of(v, eighths) for v in twice], tile)
    settle(before_edges)
    whole = slice(0, H)
    sides = side_by_side(once, 0, Y - 1, whole)
    cost_sides = side_by_side(cost, 0, Y - 1, whole)
    inner_first = side_by_side(once, 1, None, slice(0, 32))
    inner_last = side_by_side(once, None, Y - 2, slice(32, H))
    after_sides, before_sides = pltpu.roll(sides, Y - 1, 1), pltpu.roll(sides, 1, 1)
    for n in edges:
        land(n)
    last_three = reply((
        around(once, hr_m[...], hr_p[...], hc_m[...], hc_p[...], 0),
        around(once, hr_m[...], hr_p[...], hc_m[...], hc_p[...], 7),
        (
            sides, before_sides[16:48, :], (after_sides[0:16, :], after_sides[48:64, :]),
            jnp.where(lane_of < 8, inner_first, pltpu.roll(hc_p[...], 8, 1)),
            jnp.where(lane_of < 8, hc_m[...], inner_last), w_sides,
        ),
    ))
    ends = (closed(0, last_three[0]), closed(7, last_three[1]))
    columns = (cost_sides + last_three[2]) * keep_sides
    patch = columns[0:8, :]
    for n in range(1, 8):
        here = jnp.logical_and(lane_8 >= 16 * n, lane_8 < 16 * n + 16)
        patch = jnp.where(here, pltpu.roll(columns[8 * n:8 * n + 8, :], 16 * n, 1), patch)
    eighths = eighths_of(jnp.concatenate(ends, axis=0))
    eighths_patch = eighths_of(patch)
    scales = jnp.where(row_8 < 4, eighths, eighths_patch)
    inverse = (32767.0 * 8.0) / eighths_patch.astype(F32)
    patch_code = (patch * inverse + 32768.5).astype(I32) - 32768
    tile = jnp.concatenate([scales, patch_code], axis=0).astype(I16)
    gathers += send_piece(PIECES - 1, [code_of(v, eighths) for v in ends], tile)

    lane_w = lax.broadcasted_iota(I32, (H, Y), 1)
    out_rows = out.reshape(H * X, Y)

    def unpack(codes, qq, piece):
        scale = codes[MARK:MARK + 1, :].astype(F32) * (0.125 / 32767.0)
        indices = (2 * piece + 1, 2 * piece + 2) if piece < PIECES - 1 else (0, 7)
        for n, i in enumerate(indices):
            out_rows[pl.ds(qq * 8 + i, H, stride=X), :] = codes[H * n:H * n + H, :].astype(F32) * scale
        if piece < PIECES - 1:
            return
        scale = codes[MARK + 4:MARK + 5, :].astype(F32) * (0.125 / 32767.0)
        flat = codes[MARK + 8:MARK + 16, :].astype(F32) * scale
        wide = jnp.concatenate([pltpu.roll(flat, Y - 16 * n, 1) if n else flat for n in range(8)], axis=0)
        for i in range(1, 7):
            at_row = pl.ds(qq * 8 + i, H, stride=X)
            v = jnp.where(lane_w == 0, pltpu.roll(wide, Y - i, 1), out_rows[at_row, :])
            out_rows[at_row, :] = jnp.where(lane_w == Y - 1, pltpu.roll(wide, Y - 9 - i, 1), v)

    for piece in range(PIECES):
        unpack(gsend[piece].astype(I32), q, piece)
    settle(len(started) - 3)
    for n, piece, d in gathers:
        land(n)
        yy = (y + 4 - d) % 4
        unpack(grecv[piece, d - 1].astype(I32), jnp.where(odd == 1, 3 - yy, yy), piece)
    finish_all()


def write_out(moved, values, moved_out, values_out, sems):
    copies = [
        pltpu.make_async_copy(src, dst, sems.at[i])
        for i, (src, dst) in enumerate(((moved, moved_out), (values, values_out)))
    ]
    for c in copies:
        c.start()
    for c in copies:
        c.wait()


def shards(density, turn_rate, value_init, labels, counts, kernel_matrix):
    along_x, along_y, coupling = tables()
    vmem = lambda *shape: pltpu.VMEM(shape, F32)
    in_hbm = pl.BlockSpec(memory_space=pltpu.HBM)
    scratch = [
        vmem(H, X, Y), pltpu.VMEM((H, X, Y), BF16), vmem(H, X, Y), pltpu.VMEM((X, Y), I32), vmem(H, Y), vmem(H, Y),
        vmem(H, H), vmem(H, H),
        vmem(40, Y), vmem(40, Y), *[vmem(32, Y) for _ in range(6)],
        vmem(40, Y), vmem(40, Y), *[vmem(32, Y) for _ in range(6)],
        vmem(H, X, Y), vmem(4, 16, Y), vmem(4, X, Y), vmem(4, 16, Y), vmem(4, X, Y), vmem(4, X, Y),
        vmem(X, Y),
        pltpu.VMEM((CHUNKS, 3, ROWS, Y), I16), pltpu.VMEM((CHUNKS, 3, ROWS, Y), I16),
        pltpu.VMEM((CHUNKS, 2, ROWS, Y), I16), pltpu.VMEM((CHUNKS, 2, ROWS, Y), I16), vmem(512, Y), vmem(8, H, Y),
        vmem(32, Y), vmem(32, Y), vmem(8, Y), vmem(H, 128), vmem(H, 128),
        *[vmem(32, Y) for _ in range(8)],
        pltpu.VMEM((PIECES, MARK + 16, Y), I16), pltpu.VMEM((PIECES, 3, MARK + 16, Y), I16),
        pltpu.SMEM((16,), I32), pltpu.SemaphoreType.REGULAR((3,)), pltpu.SemaphoreType.DMA((12,)),
        pltpu.SemaphoreType.DMA((COPIES,)), pltpu.SemaphoreType.DMA((COPIES,)),
    ]
    held = pltpu.VMEM((H, X, Y), F32)
    in_vmem = pl.BlockSpec(memory_space=pltpu.VMEM)
    operands = (
        counts, density[0], turn_rate[0], value_init, labels,
        jnp.asarray(along_x), jnp.asarray(along_y), jnp.asarray(coupling), kernel_matrix,
    )
    moved, values = pl.pallas_call(
        kernel,
        out_shape=(held, held),
        in_specs=[in_hbm] * 9,
        out_specs=(in_vmem, in_vmem),
        scratch_shapes=scratch,
        compiler_params=pltpu.CompilerParams(
            collective_id=1, has_side_effects=True, vmem_limit_bytes=40 * 1024 * 1024
        ),
        name="play",
    )(*[pltpu.with_memory_space_constraint(a, pltpu.HBM) for a in operands])
    whole = jax.ShapeDtypeStruct((H, X, Y), F32)
    moved, values = pl.pallas_call(
        write_out,
        out_shape=(whole, whole),
        in_specs=[in_vmem, in_vmem],
        out_specs=(in_hbm, in_hbm),
        scratch_shapes=[pltpu.SemaphoreType.DMA((2,))],
        compiler_params=pltpu.CompilerParams(vmem_limit_bytes=8 * 1024 * 1024),
        name="write",
    )(moved, values)
    return moved[None], values


def solution(mesh):
    placed = (
        P("member", None, "gx", "gy"),
        P("member", None, "gx", "gy"),
        P(None, "gx", "gy"),
        P("gx", "gy"),
        P(),
        P(),
    )
    return jax.shard_map(
        shards,
        mesh=mesh,
        in_specs=placed,
        out_specs=(P("member", None, "gx", "gy"), P(None, "gx", "gy")),
        check_vma=False,
    )
```

```python
import jax
import jax.numpy as jnp
import numpy as np
from jax import lax
from jax.experimental import pallas as pl
from jax.experimental.pallas import tpu as pltpu
from jax.sharding import PartitionSpec as P

MESH = pl.DeviceIdType.MESH
F32 = jnp.float32
BF16 = jnp.bfloat16
I16 = jnp.int16
I32 = jnp.int32

H, X, Y = 64, 32, 128
SPEED = 0.55
BOUND = 9.5

ROW_UP, ROW_DOWN, COL_UP, COL_DOWN, VAL_UP, VAL_DOWN, VALCOL_UP, VALCOL_DOWN = range(8)
CHUNK = 8
CHUNKS = H // CHUNK
ROWS = 8 * CHUNK
STEP_ROW, STEP_COL, OVER_Y = 8, 12, 16
OVER_Z = OVER_Y + 3 * CHUNKS
REPLY = OVER_Z + 2 * CHUNKS
GATHER = REPLY + 4
PIECES = 4
SPAN = 8 // PIECES
MARK = H * SPAN
COPIES = GATHER + 3 * PIECES


def tables():
    angles = np.arange(H, dtype=np.float32) * np.float32(2.0 * np.pi / H)
    along_x = np.abs(SPEED * np.cos(angles)).astype(np.float32)
    along_y = np.abs(SPEED * np.sin(angles)).astype(np.float32)
    spread = angles[:, None] - angles[None, :]
    coupling = np.exp(-5.0 * (1.0 - np.cos(spread.astype(np.float64)))).astype(np.float32)
    wide = lambda v: np.ascontiguousarray(np.broadcast_to(v[:, None], (H, Y)))
    return wide(along_x), wide(along_y), coupling


def encode(x):
    root = jnp.sqrt(jnp.maximum(x, 0.0)) * 65535.0 + 0.5
    return (root.astype(I32) - 32768).astype(I16)


def decode(code):
    root = code.astype(I32).astype(F32) + 32768.0
    return root * root * (BOUND / (65535.0 * 65535.0))


def split_left(m):
    high = m.astype(BF16)
    low = (m - high.astype(F32)).astype(BF16)
    return high, low


def widen(m):
    high, low = split_left(m)
    return jnp.concatenate([high, low, high, low], axis=0)


def kernel(
    counts_hbm, density, turn_hbm, value_hbm, labels_hbm, ax_hbm, ay_hbm, coupling_hbm, kernel_hbm,
    r2, out,
    r0, turn, val, labels, axt, ayt, coupling, kern,
    sx_m, sx_p, sy_m, sy_p, sv_m, sv_p, svc_m, svc_p, hx_m, hx_p, hy_m, hy_p, hv_m, hv_p, hvc_m, hvc_p,
    r1, s2x, s2y, h2x, h2y, weights, keep,
    ysend, yrecv, zsend, zrecv, total, base,
    up_row, down_row, cs, kf, cf,
    sr_m, sr_p, sc_m, sc_p, hr_m, hr_p, hc_m, hc_p,
    gsend, grecv,
    counts, word, word_y, load_sem, ss, rs,
):
    member = lax.axis_index("member")
    gx = lax.axis_index("gx")
    gy = lax.axis_index("gy")
    zh, y = member // 4, member % 4
    odd = gx % 2
    q = jnp.where(odd == 1, 3 - y, y)
    turn_sign = jnp.where(odd == 1, 3, 1)

    def at(z, yy):
        return {"member": z * 4 + yy}

    pair = (jnp.where(zh % 2 == 0, zh + 1, zh - 1), 3 - zh)

    quads = [pl.ds(16 * k, 16) for k in (0, 3, 1, 2)]
    loads = [
        pltpu.make_async_copy(src, dst, load_sem.at[i])
        for i, (src, dst) in enumerate((
            *[(density.at[b], r0.at[b]) for b in quads],
            (labels_hbm, labels), (turn_hbm, turn), (value_hbm, val), (ax_hbm, axt), (ay_hbm, ayt),
            (coupling_hbm, coupling), (kernel_hbm, kern), (counts_hbm, counts),
        ))
    ]
    for c in loads[:5]:
        c.start()

    barrier = pltpu.get_barrier_semaphore()
    z_lo, core = gx // 2, gx % 2
    z_up, z_down = (zh * 4 + z_lo + 1) % 16, (zh * 4 + z_lo + 15) % 16
    beside = [{"member": (z // 4) * 4 + y, "gx": (z % 4) * 2 + core} for z in (z_up, z_down)]
    beside_y = [at(zh, (y + d) % 4) for d in (1, 3)]
    greeted = beside_y + beside
    greeted += [{"gy": (gy + d) % 4} for d in (1, 3)]

    def greet(target):
        pl.semaphore_signal(barrier, inc=1, device_id=target, device_id_type=MESH)

    has_m, has_p = gx > 0, gx < 7
    west, east = gy > 0, gy < 3
    to_m, to_p = {"gx": (gx + 7) % 8}, {"gx": (gx + 1) % 8}
    to_w, to_e = {"gy": (gy + 3) % 4}, {"gy": (gy + 1) % 4}
    pl.when(has_m)(lambda: greet(to_m))
    pl.when(has_p)(lambda: greet(to_p))
    for target in greeted:
        greet(target)

    for c in loads[5:]:
        c.start()

    def copy(i, src, dst, target):
        return pltpu.make_async_remote_copy(
            src_ref=src, dst_ref=dst, send_sem=ss.at[i], recv_sem=rs.at[i], device_id=target, device_id_type=MESH
        )

    lane = lax.broadcasted_iota(I32, (X, Y), 1)
    row = lax.broadcasted_iota(I32, (X, Y), 0)
    lane_h = lax.broadcasted_iota(I32, (32, Y), 1)

    def shift_x(r, halo, k):
        if k in (0, 3):
            return jnp.where(row == 0, halo, pltpu.roll(r, 1, 0))
        return jnp.where(row == X - 1, halo, pltpu.roll(r, X - 1, 0))

    def shift_y(r, halo, position, k):
        if k in (0, 1):
            moved_halo = pltpu.roll(halo, lax.rem(Y - position, Y), 1)
            return jnp.where(lane == 0, moved_halo, pltpu.roll(r, 1, 1))
        moved_halo = pltpu.roll(halo, Y - 1 - position, 1)
        return jnp.where(lane == Y - 1, moved_halo, pltpu.roll(r, Y - 1, 1))

    def pack_column(acc, r, position, k):
        shift = position + 1 if k in (0, 1) else position
        return jnp.where(lane == position, pltpu.roll(r, shift, 1), acc)

    for c in loads[:5]:
        c.wait()
    opened = jnp.where(labels[...] != 1, 1.0, 0.0).astype(F32)
    keep[...] = jnp.where(labels[...] == 2, 0.0, 1.0).astype(F32)
    zero_plane = jnp.zeros((X, Y), F32)

    def rows_of(ref, h0, n, x):
        return ref.reshape(H * X, Y)[pl.ds(h0 * X + x, n, stride=X), :]

    sx_p[0:16, :] = rows_of(r0, 0, 16, X - 1)
    sx_p[16:32, :] = rows_of(r0, 48, 16, X - 1)
    sx_p[32:40, :] = jnp.broadcast_to(opened[X - 1:X, :], (8, Y))
    sx_m[0:32, :] = rows_of(r0, 16, 32, 0)
    sx_m[32:40, :] = jnp.broadcast_to(opened[0:1, :], (8, Y))

    for k0, dst, shift in ((0, sy_p, 65), (2, sy_m, 64)):
        def pack(j, acc, k0=k0):
            return pack_column(acc, r0[k0 * 16 + j], j, k0)
        acc = lax.fori_loop(0, 32, pack, zero_plane, unroll=32)
        dst[...] = jnp.where(lane == 64, pltpu.roll(opened, shift, 1), acc)

    def value_row(i):
        return val.reshape(H * X, Y)[pl.ds(q * 8 + i, H, stride=X), :]

    def pack_values(rows, headings, side):
        acc = jnp.zeros((32, Y), F32)
        for i in range(8):
            part = rows[i][headings:headings + 32, :]
            shift = i + 1 if side else i
            acc = jnp.where(lane_h == i, pltpu.roll(part, shift, 1) if shift else part, acc)
        return acc

    low, high = q == 0, q == 3
    near_up = {"member": zh * 4 + jnp.where(low, y, (y + 4 - turn_sign) % 4), "gx": jnp.where(low, (gx + 7) % 8, gx)}
    near_down = {"member": zh * 4 + jnp.where(high, y, (y + turn_sign) % 4), "gx": jnp.where(high, (gx + 1) % 8, gx)}
    has_up, has_down = jnp.logical_or(q > 0, has_m), jnp.logical_or(q < 3, has_p)

    first = (
        (copy(ROW_DOWN, sx_p, hx_m, to_p), has_p, has_m),
        (copy(ROW_UP, sx_m, hx_p, to_m), has_m, has_p),
        (copy(COL_DOWN, sy_p, hy_m, to_e), east, west),
        (copy(COL_UP, sy_m, hy_p, to_w), west, east),
        (copy(VAL_DOWN, sv_p, hv_m, to_p), jnp.logical_and(high, has_p), jnp.logical_and(low, has_m)),
        (copy(VAL_UP, sv_m, hv_p, to_m), jnp.logical_and(low, has_m), jnp.logical_and(high, has_p)),
        (copy(VALCOL_DOWN, svc_p, hvc_m, to_e), east, west),
        (copy(VALCOL_UP, svc_m, hvc_p, to_w), west, east),
    )

    started, landed = [], set()

    def guarded(condition, act):
        if condition is True:
            act()
        else:
            pl.when(condition)(act)

    def launch(c, sends=True, receives=True):
        guarded(sends, c.start)
        started.append((c, sends, receives))
        return len(started) - 1

    def land(n):
        c, _, receives = started[n]
        guarded(receives, c.wait_recv)
        landed.add(n)

    sent = set()

    def settle(upto):
        for n in range(upto):
            if n not in sent:
                c, sends, _ = started[n]
                guarded(sends, c.wait_send)
                sent.add(n)

    def finish_all():
        for n in range(len(started)):
            if n not in landed:
                land(n)
        settle(len(started))

    pl.semaphore_wait(barrier, len(greeted) + has_m.astype(I32) + has_p.astype(I32))

    def pass_word(n):
        for target in beside:
            pl.semaphore_signal(word.at[n], inc=1, device_id=target, device_id_type=MESH)

    pass_word(0)
    for target in beside_y:
        pl.semaphore_signal(word_y, inc=1, device_id=target, device_id_type=MESH)
    begun = [launch(*c) for c in first[:4]]
    @pl.when(gx == 0)
    def _():
        hx_m[...] = jnp.zeros((40, Y), F32)
        hv_m[...] = jnp.zeros((32, Y), F32)
        for k in (0, 3):
            h2x[k] = jnp.zeros((16, Y), F32)

    @pl.when(gx == 7)
    def _():
        hx_p[...] = jnp.zeros((40, Y), F32)
        hv_p[...] = jnp.zeros((32, Y), F32)
        for k in (1, 2):
            h2x[k] = jnp.zeros((16, Y), F32)

    @pl.when(gy == 0)
    def _():
        for ref in (hy_m, h2y.at[0], h2y.at[1], hvc_m, hc_m):
            ref[...] = zero_plane

    @pl.when(gy == 3)
    def _():
        for ref in (hy_p, h2y.at[2], h2y.at[3], hvc_p, hc_p):
            ref[...] = zero_plane

    @pl.when(jnp.logical_not(has_up))
    def _():
        hr_m[...] = jnp.zeros((32, Y), F32)

    @pl.when(jnp.logical_not(has_down))
    def _():
        hr_p[...] = jnp.zeros((32, Y), F32)

    loads[6].wait()
    own = [value_row(i) for i in range(8)]
    svc_p[...] = pack_values(own, 32, True)
    svc_m[...] = pack_values(own, 0, False)
    sv_p[...] = own[7][16:48, :]
    sv_m[0:16, :] = own[0][0:16, :]
    sv_m[16:32, :] = own[0][48:64, :]
    begun += [launch(*c) for c in first[4:]]
    for n in (5, 7, 8, 9, 10, 11):
        loads[n].wait()
    kf[:, 0:64] = kern[...]
    kf[:, 64:128] = kern[...]
    for n in begun[:4]:
        land(n)

    open_p = jnp.where(row == X - 1, hx_p[32:33, :], pltpu.roll(opened, X - 1, 0))
    open_m = jnp.where(row == 0, hx_m[32:33, :], pltpu.roll(opened, 1, 0))
    open_e = jnp.where(lane == Y - 1, pltpu.roll(hy_p[...], 63, 1), pltpu.roll(opened, Y - 1, 1))
    open_w = jnp.where(lane == 0, pltpu.roll(hy_m[...], 64, 1), pltpu.roll(opened, 1, 1))
    weights[0] = opened * open_p
    weights[1] = opened * open_m
    weights[2] = opened * open_e
    weights[3] = opened * open_w

    def transport(k, src, dst, halo_x, x_at, halo_y, y_at, packed):
        out_x, in_x = (0, 1) if k in (0, 3) else (1, 0)
        out_y, in_y = (2, 3) if k in (0, 1) else (3, 2)
        wox, wix, woy, wiy = weights[out_x], weights[in_x], weights[out_y], weights[in_y]
        kept = keep[...]
        columns = halo_y[...]
        h0 = 16 * k

        def turns(h):
            r = src[h]
            t = turn[h].astype(F32)
            up = jnp.maximum(t, 0.0) * r
            return r, up, up - t * r

        def start_of(j):
            h = h0 + j
            r, up, down = turns(h)
            ax = axt[pl.ds(h, 1), :]
            ay = ayt[pl.ds(h, 1), :]
            hx = halo_x[pl.ds(x_at + j, 1), :]
            xn = shift_x(r, hx, k)
            yn = shift_y(r, columns, y_at + j, k)
            s = r - up - down + ax * (wix * xn - wox * r) + ay * (wiy * yn - woy * r)
            return s, up, down

        _, up_before, _ = turns((h0 + 63) % 64)
        s, up, _ = start_of(0)
        carry = (s + up_before, up, zero_plane if packed is None else packed)

        def finish(j, partial, down, acc):
            new = (partial + down) * kept
            dst[h0 + j] = new
            return acc if packed is None else pack_column(acc, new, y_at + j, k)

        def body(j, carry):
            partial, up_last, acc = carry
            s, up, down = start_of(j)
            acc = finish(j - 1, partial, down, acc)
            return s + up_last, up, acc

        partial, _, acc = lax.fori_loop(1, 16, body, carry, unroll=15)
        _, _, down = turns((h0 + 16) % 64)
        return finish(15, partial, down, acc)

    def halos(k, row_m, row_p, column_m, column_p):
        return (
            ((row_m, 0), (row_p, 0), (row_p, 16), (row_m, 16))[k]
            + ((column_m, 0), (column_m, 16), (column_p, 0), (column_p, 16))[k]
        )

    second = []
    for k in range(4):
        s2y[k] = transport(k, r0, r1, *halos(k, hx_m, hx_p, hy_m, hy_p), zero_plane)
        s2x[k] = rows_of(r1, 16 * k, 16, X - 1 if k in (0, 3) else 0)
        target = (to_p, has_p, has_m) if k in (0, 3) else (to_m, has_m, has_p)
        second.append(launch(copy(STEP_ROW + k, s2x.at[k], h2x.at[k], target[0]), *target[1:]))
        target = (to_e, east, west) if k in (0, 1) else (to_w, west, east)
        second.append(launch(copy(STEP_COL + k, s2y.at[k], h2y.at[k], target[0]), *target[1:]))

    pl.semaphore_wait(word_y, 2)
    pl.semaphore_wait(word.at[0], 2)
    pass_word(1)

    over_y = [[] for _ in range(CHUNKS)]
    for k in range(4):
        for n in second[2 * k:2 * k + 2]:
            land(n)
        transport(k, r1, r2, h2x.at[k], 0, h2y.at[k], (0, 16, 0, 16)[k], None)
        for c in range(k * CHUNKS // 4, (k + 1) * CHUNKS // 4):
            for d in (2, 1, 3):
                yy = (y + d) % 4
                qq = jnp.where(odd == 1, 3 - yy, yy)
                part = r2[pl.ds(CHUNK * c, CHUNK), pl.ds(pl.multiple_of(qq * 8, 8), 8), :]
                ysend[c, d - 1] = encode(part.reshape(ROWS, Y) * (1.0 / BOUND))
                there = copy(OVER_Y + 3 * c + d - 1, ysend.at[c, d - 1], yrecv.at[c, d - 1], at(zh, yy))
                over_y[c].append(launch(there))
    pl.semaphore_wait(word.at[1], 2)
    pass_word(2)

    def count(z, yy):
        return counts[z * 4 + yy].astype(F32)

    def plane_of(scalar):
        return jnp.full((8, Y), scalar, F32)

    def group(z):
        return count(z, 0) + count(z, 1) + count(z, 2) + count(z, 3)

    mine, across = group(zh), [group(p) for p in pair]
    everyone = group(0) + group(1) + group(2) + group(3)
    inverse_all = 1.0 / plane_of(everyone)
    inverse_mine = (1.0 / BOUND) / plane_of(mine)

    def scaled(part, factor):
        return (part.reshape(CHUNK, 8, Y) * factor).reshape(ROWS, Y)

    pl.semaphore_wait(word.at[2], 2)
    over_z = [[None, None] for _ in range(CHUNKS)]
    for c in range(CHUNKS):
        block = pl.ds(CHUNK * c, CHUNK)
        part = r2[block, pl.ds(pl.multiple_of(q * 8, 8), 8), :].reshape(ROWS, Y) * count(zh, y)
        for n, d in zip(over_y[c], (2, 1, 3)):
            land(n)
            part = part + decode(yrecv[c, d - 1]) * count(zh, (y + 4 - d) % 4)
        zsend[c, 0] = encode(scaled(part, inverse_mine))
        over_z[c][0] = launch(copy(OVER_Z + 2 * c, zsend.at[c, 0], zrecv.at[c, 0], at(pair[c % 2], y)))

    for n in begun[4:]:
        land(n)

    @pl.when(low)
    def _():
        up_row[...] = hv_m[...]

    @pl.when(q > 0)
    def _():
        up_row[...] = val.reshape(H * X, Y)[pl.ds(16 * X + q * 8 - 1, 32, stride=X), :]

    @pl.when(high)
    def _():
        down_row[...] = hv_p[...]

    @pl.when(q < 3)
    def _():
        down_row[0:16, :] = val.reshape(H * X, Y)[pl.ds(q * 8 + 8, 16, stride=X), :]
        down_row[16:32, :] = val.reshape(H * X, Y)[pl.ds(48 * X + q * 8 + 8, 16, stride=X), :]

    wide_rows = pl.ds(pl.multiple_of(q * 8, 8), 8)
    w_rows = [weights[i, wide_rows, :] for i in range(4)]
    keep_rows = keep[wide_rows, :]
    kf_high, kf_low = split_left(kf[...])
    lane_c = lax.broadcasted_iota(I32, (64, 2 * Y), 1)
    kb = jnp.concatenate([kf_high, kf_low], axis=1)
    cf[:, 0:64] = coupling[...]
    cf[:, 64:128] = coupling[...]
    cf_high, cf_low = split_left(cf[...])
    cb = jnp.concatenate([cf_high, cf_low], axis=1)

    lane_of = lax.broadcasted_iota(I32, (32, Y), 1)

    def around(rows, before, after, first_column, last_column, i):
        v = rows[i]
        prior = rows[i - 1][16:48, :] if i > 0 else before
        if i < 7:
            later = (rows[i + 1][0:16, :], rows[i + 1][48:64, :])
        else:
            later = (after[0:16, :], after[16:32, :])
        north, south = pltpu.roll(v[0:32, :], Y - 1, 1), pltpu.roll(v[32:64, :], 1, 1)
        if last_column is not None:
            north = jnp.where(lane_of == Y - 1, pltpu.roll(last_column, Y - 1 - i, 1), north)
            south = jnp.where(lane_of == 0, pltpu.roll(first_column, Y - i, 1) if i else first_column, south)
        return v, prior, later, north, south, [w[i:i + 1, :] for w in w_rows]

    def reply(jobs):
        lowest_of, parts = [], []
        for v, prior, later, north, south, w in jobs:
            moves = []
            for k in range(4):
                part = slice(16 * k, 16 * k + 16)
                vk = v[part, :]
                xn = (later[0], prior[0:16, :], prior[16:32, :], later[1])[k]
                yn = (north[0:16, :], north[16:32, :], south[0:16, :], south[16:32, :])[k]
                wx = w[0 if k in (0, 3) else 1]
                wy = w[2 if k in (0, 1) else 3]
                moves.append(vk + axt[part, :] * (wx * (xn - vk)) + ayt[part, :] * (wy * (yn - vk)))
            moves = jnp.concatenate(moves, axis=0)
            lowest = jnp.min(moves, axis=0, keepdims=True)
            lowest_of.append(lowest)
            parts.append(jnp.exp((lowest - moves) * 10.0))
        summed = jnp.dot(cb, widen(jnp.concatenate(parts, axis=1)), preferred_element_type=F32)
        logs = jnp.log(summed) * 0.1
        return [lowest_of[n] - logs[:, n * Y:(n + 1) * Y] for n in range(len(jobs))]

    row_8 = lax.broadcasted_iota(I32, (8, Y), 0)
    lane_8 = lax.broadcasted_iota(I32, (8, Y), 1)

    def sides_of(w):
        first = jnp.where(lane_8 == row_8, w[:, 0:1], 0.0)
        last = jnp.where(lane_8 == row_8 + 8, w[:, Y - 1:Y], 0.0)
        return jnp.sum(first + last, axis=0, keepdims=True)

    w_sides = [sides_of(w) for w in w_rows]
    keep_sides = sides_of(keep_rows)

    def side_by_side(rows, first, last, part):
        acc = jnp.zeros((part.stop - part.start, Y), F32)
        lanes = lax.broadcasted_iota(I32, acc.shape, 1)
        for i in range(8):
            if first is not None:
                acc = jnp.where(lanes == i, pltpu.roll(rows[i][part, :], (i - first) % Y, 1), acc)
            if last is not None:
                acc = jnp.where(lanes == 8 + i, pltpu.roll(rows[i][part, :], (8 + i - last) % Y, 1), acc)
        return acc

    from_start = reply([around(own, up_row[...], down_row[...], hvc_m[...], hvc_p[...], i) for i in range(8)])
    for i in range(8):
        base[i] = from_start[i]

    lower = [jnp.full((8, Y), zh, I32) < jnp.full((8, Y), p, I32) for p in pair]

    def merge(c, stage, partner, weight_own, weight_other):
        a = decode(zsend[c, stage]).reshape(CHUNK, 8, Y) * weight_own
        b = decode(zrecv[c, stage]).reshape(CHUNK, 8, Y) * weight_other
        is_low = lower[partner]
        return jnp.where(is_low, a, b) + jnp.where(is_low, b, a)

    factors = [(1.0 / BOUND) / plane_of(mine + across[p]) for p in range(2)]
    for c in range(CHUNKS):
        p = c % 2
        land(over_z[c][0])
        both = merge(c, 0, p, mine, across[p])
        zsend[c, 1] = encode((both * factors[p]).reshape(ROWS, Y))
        over_z[c][1] = launch(copy(OVER_Z + 2 * c + 1, zsend.at[c, 1], zrecv.at[c, 1], at(pair[1 - p], y)))
    for c in range(CHUNKS):
        p = c % 2
        land(over_z[c][1])
        here = mine + across[p]
        mixed = merge(c, 1, 1 - p, here, everyone - here) * inverse_all
        total[pl.ds(ROWS * c, ROWS), :] = mixed.reshape(ROWS, Y)

    mixed_rows = jnp.concatenate([total[pl.ds(i, H, stride=8), :] for i in range(8)], axis=1)
    running = 0.5 + 0.5 * jnp.dot(kb, widen(mixed_rows), preferred_element_type=F32)
    cost = [running[:, i * Y:(i + 1) * Y] for i in range(8)]
    once = [(cost[i] + base[i]) * keep_rows[i:i + 1, :] for i in range(8)]

    sr_p[...] = once[7][16:48, :]
    sr_m[0:16, :] = once[0][0:16, :]
    sr_m[16:32, :] = once[0][48:64, :]
    before_edges = len(started)
    edges = [
        launch(copy(REPLY, sr_p, hr_m, near_down), has_down, has_up),
        launch(copy(REPLY + 1, sr_m, hr_p, near_up), has_up, has_down),
    ]
    sc_p[...] = pack_values(once, 32, True)
    edges.append(launch(copy(REPLY + 2, sc_p, hc_m, to_e), east, west))
    sc_m[...] = pack_values(once, 0, False)
    edges.append(launch(copy(REPLY + 3, sc_m, hc_p, to_w), west, east))

    def code_of(v, eighths):
        inverse = (32767.0 * 8.0) / eighths.astype(F32)
        return ((v * inverse + 32768.5).astype(I32) - 32768).astype(I16)

    def eighths_of(v):
        return (jnp.max(jnp.abs(v), axis=0, keepdims=True) * 8.0).astype(I32) + 1

    def send_piece(piece, rows, tile):
        for n in range(SPAN):
            gsend[piece, pl.ds(H * n, H), :] = rows[n]
        gsend[piece, pl.ds(MARK, 16), :] = tile
        out = []
        for d in (2, 1, 3):
            there = copy(GATHER + 3 * piece + d - 1, gsend.at[piece], grecv.at[piece, d - 1], at(zh, (y + d) % 4))
            out.append((launch(there), piece, d))
        return out

    def closed(i, t):
        return (cost[i] + t) * keep_rows[i:i + 1, :]

    gathers = []
    for piece in range(PIECES - 1):
        indices = (2 * piece + 1, 2 * piece + 2)
        twice = [closed(i, t) for i, t in zip(indices, reply([around(once, None, None, None, None, i) for i in indices]))]
        eighths = eighths_of(jnp.concatenate(twice, axis=0))
        tile = jnp.broadcast_to(eighths, (16, Y)).astype(I16)
        gathers += send_piece(piece, [code_of(v, eighths) for v in twice], tile)
    settle(before_edges)
    whole = slice(0, H)
    sides = side_by_side(once, 0, Y - 1, whole)
    cost_sides = side_by_side(cost, 0, Y - 1, whole)
    inner_first = side_by_side(once, 1, None, slice(0, 32))
    inner_last = side_by_side(once, None, Y - 2, slice(32, H))
    after_sides, before_sides = pltpu.roll(sides, Y - 1, 1), pltpu.roll(sides, 1, 1)
    for n in edges:
        land(n)
    last_three = reply((
        around(once, hr_m[...], hr_p[...], hc_m[...], hc_p[...], 0),
        around(once, hr_m[...], hr_p[...], hc_m[...], hc_p[...], 7),
        (
            sides, before_sides[16:48, :], (after_sides[0:16, :], after_sides[48:64, :]),
            jnp.where(lane_of < 8, inner_first, pltpu.roll(hc_p[...], 8, 1)),
            jnp.where(lane_of < 8, hc_m[...], inner_last), w_sides,
        ),
    ))
    ends = (closed(0, last_three[0]), closed(7, last_three[1]))
    columns = (cost_sides + last_three[2]) * keep_sides
    patch = columns[0:8, :]
    for n in range(1, 8):
        here = jnp.logical_and(lane_8 >= 16 * n, lane_8 < 16 * n + 16)
        patch = jnp.where(here, pltpu.roll(columns[8 * n:8 * n + 8, :], 16 * n, 1), patch)
    eighths = eighths_of(jnp.concatenate(ends, axis=0))
    eighths_patch = eighths_of(patch)
    scales = jnp.where(row_8 < 4, eighths, eighths_patch)
    inverse = (32767.0 * 8.0) / eighths_patch.astype(F32)
    patch_code = (patch * inverse + 32768.5).astype(I32) - 32768
    tile = jnp.concatenate([scales, patch_code], axis=0).astype(I16)
    gathers += send_piece(PIECES - 1, [code_of(v, eighths) for v in ends], tile)

    lane_w = lax.broadcasted_iota(I32, (H, Y), 1)
    out_rows = out.reshape(H * X, Y)

    def unpack(codes, qq, piece):
        scale = codes[MARK:MARK + 1, :].astype(F32) * (0.125 / 32767.0)
        indices = (2 * piece + 1, 2 * piece + 2) if piece < PIECES - 1 else (0, 7)
        for n, i in enumerate(indices):
            out_rows[pl.ds(qq * 8 + i, H, stride=X), :] = codes[H * n:H * n + H, :].astype(F32) * scale
        if piece < PIECES - 1:
            return
        scale = codes[MARK + 4:MARK + 5, :].astype(F32) * (0.125 / 32767.0)
        flat = codes[MARK + 8:MARK + 16, :].astype(F32) * scale
        wide = jnp.concatenate([pltpu.roll(flat, Y - 16 * n, 1) if n else flat for n in range(8)], axis=0)
        for i in range(1, 7):
            at_row = pl.ds(qq * 8 + i, H, stride=X)
            v = jnp.where(lane_w == 0, pltpu.roll(wide, Y - i, 1), out_rows[at_row, :])
            out_rows[at_row, :] = jnp.where(lane_w == Y - 1, pltpu.roll(wide, Y - 9 - i, 1), v)

    for piece in range(PIECES):
        unpack(gsend[piece].astype(I32), q, piece)
    settle(len(started) - 3)
    for n, piece, d in sorted(gathers, key=lambda g: (g[1], g[2] == 2)):
        land(n)
        yy = (y + 4 - d) % 4
        unpack(grecv[piece, d - 1].astype(I32), jnp.where(odd == 1, 3 - yy, yy), piece)
    finish_all()


def write_out(moved, values, moved_out, values_out, sems):
    copies = [
        pltpu.make_async_copy(src, dst, sems.at[i])
        for i, (src, dst) in enumerate(((moved, moved_out), (values, values_out)))
    ]
    for c in copies:
        c.start()
    for c in copies:
        c.wait()


def shards(density, turn_rate, value_init, labels, counts, kernel_matrix):
    along_x, along_y, coupling = tables()
    vmem = lambda *shape: pltpu.VMEM(shape, F32)
    in_hbm = pl.BlockSpec(memory_space=pltpu.HBM)
    scratch = [
        vmem(H, X, Y), pltpu.VMEM((H, X, Y), BF16), vmem(H, X, Y), pltpu.VMEM((X, Y), I32), vmem(H, Y), vmem(H, Y),
        vmem(H, H), vmem(H, H),
        vmem(40, Y), vmem(40, Y), *[vmem(32, Y) for _ in range(6)],
        vmem(40, Y), vmem(40, Y), *[vmem(32, Y) for _ in range(6)],
        vmem(H, X, Y), vmem(4, 16, Y), vmem(4, X, Y), vmem(4, 16, Y), vmem(4, X, Y), vmem(4, X, Y),
        vmem(X, Y),
        pltpu.VMEM((CHUNKS, 3, ROWS, Y), I16), pltpu.VMEM((CHUNKS, 3, ROWS, Y), I16),
        pltpu.VMEM((CHUNKS, 2, ROWS, Y), I16), pltpu.VMEM((CHUNKS, 2, ROWS, Y), I16), vmem(512, Y), vmem(8, H, Y),
        vmem(32, Y), vmem(32, Y), vmem(8, Y), vmem(H, 128), vmem(H, 128),
        *[vmem(32, Y) for _ in range(8)],
        pltpu.VMEM((PIECES, MARK + 16, Y), I16), pltpu.VMEM((PIECES, 3, MARK + 16, Y), I16),
        pltpu.SMEM((16,), I32), pltpu.SemaphoreType.REGULAR((3,)), pltpu.SemaphoreType.REGULAR, pltpu.SemaphoreType.DMA((12,)),
        pltpu.SemaphoreType.DMA((COPIES,)), pltpu.SemaphoreType.DMA((COPIES,)),
    ]
    held = pltpu.VMEM((H, X, Y), F32)
    in_vmem = pl.BlockSpec(memory_space=pltpu.VMEM)
    operands = (
        counts, density[0], turn_rate[0], value_init, labels,
        jnp.asarray(along_x), jnp.asarray(along_y), jnp.asarray(coupling), kernel_matrix,
    )
    moved, values = pl.pallas_call(
        kernel,
        out_shape=(held, held),
        in_specs=[in_hbm] * 9,
        out_specs=(in_vmem, in_vmem),
        scratch_shapes=scratch,
        compiler_params=pltpu.CompilerParams(
            collective_id=1, has_side_effects=True, vmem_limit_bytes=40 * 1024 * 1024
        ),
        name="play",
    )(*[pltpu.with_memory_space_constraint(a, pltpu.HBM) for a in operands])
    whole = jax.ShapeDtypeStruct((H, X, Y), F32)
    moved, values = pl.pallas_call(
        write_out,
        out_shape=(whole, whole),
        in_specs=[in_vmem, in_vmem],
        out_specs=(in_hbm, in_hbm),
        scratch_shapes=[pltpu.SemaphoreType.DMA((2,))],
        compiler_params=pltpu.CompilerParams(vmem_limit_bytes=8 * 1024 * 1024),
        name="write",
    )(moved, values)
    return moved[None], values


def solution(mesh):
    placed = (
        P("member", None, "gx", "gy"),
        P("member", None, "gx", "gy"),
        P(None, "gx", "gy"),
        P("gx", "gy"),
        P(),
        P(),
    )
    return jax.shard_map(
        shards,
        mesh=mesh,
        in_specs=placed,
        out_specs=(P("member", None, "gx", "gy"), P(None, "gx", "gy")),
        check_vma=False,
    )
```

```python
import jax
import jax.numpy as jnp
import numpy as np
from jax import lax
from jax.experimental import pallas as pl
from jax.experimental.pallas import tpu as pltpu
from jax.sharding import PartitionSpec as P

MESH = pl.DeviceIdType.MESH
F32 = jnp.float32
BF16 = jnp.bfloat16
I16 = jnp.int16
I32 = jnp.int32

H, X, Y = 64, 32, 128
SPEED = 0.55
BOUND = 9.5

ROW_UP, ROW_DOWN, COL_UP, COL_DOWN, VAL_UP, VAL_DOWN, VALCOL_UP, VALCOL_DOWN = range(8)
CHUNK = 8
CHUNKS = H // CHUNK
ROWS = 8 * CHUNK
STEP_ROW, STEP_COL, OVER_Y = 8, 12, 16
OVER_Z = OVER_Y + 3 * CHUNKS
REPLY = OVER_Z + 2 * CHUNKS
GATHER = REPLY + 4
PIECES = 4
SPAN = 8 // PIECES
MARK = H * SPAN
COPIES = GATHER + 3 * PIECES


def tables():
    angles = np.arange(H, dtype=np.float32) * np.float32(2.0 * np.pi / H)
    along_x = np.abs(SPEED * np.cos(angles)).astype(np.float32)
    along_y = np.abs(SPEED * np.sin(angles)).astype(np.float32)
    spread = angles[:, None] - angles[None, :]
    coupling = np.exp(-5.0 * (1.0 - np.cos(spread.astype(np.float64)))).astype(np.float32)
    wide = lambda v: np.ascontiguousarray(np.broadcast_to(v[:, None], (H, Y)))
    return wide(along_x), wide(along_y), coupling


def encode(x):
    root = jnp.sqrt(jnp.maximum(x, 0.0)) * 65535.0 + 0.5
    return (root.astype(I32) - 32768).astype(I16)


def decode(code):
    root = code.astype(I32).astype(F32) + 32768.0
    return root * root * (BOUND / (65535.0 * 65535.0))


def split_left(m):
    high = m.astype(BF16)
    low = (m - high.astype(F32)).astype(BF16)
    return high, low


def widen(m):
    high, low = split_left(m)
    return jnp.concatenate([high, low, high, low], axis=0)


def kernel(
    counts_hbm, density, turn_hbm, value_hbm, labels_hbm, ax_hbm, ay_hbm, coupling_hbm, kernel_hbm,
    r2, out,
    r0, turn, val, labels, axt, ayt, coupling, kern,
    sx_m, sx_p, sy_m, sy_p, sv_m, sv_p, svc_m, svc_p, hx_m, hx_p, hy_m, hy_p, hv_m, hv_p, hvc_m, hvc_p,
    r1, s2x, s2y, h2x, h2y, weights, keep,
    ysend, yrecv, zsend, zrecv, total, base,
    up_row, down_row, cs, kf, cf,
    sr_m, sr_p, sc_m, sc_p, hr_m, hr_p, hc_m, hc_p,
    gsend, grecv,
    counts, word, word_y, load_sem, ss, rs,
):
    member = lax.axis_index("member")
    gx = lax.axis_index("gx")
    gy = lax.axis_index("gy")
    zh, y = member // 4, member % 4
    odd = gx % 2
    q = jnp.where(odd == 1, 3 - y, y)
    turn_sign = jnp.where(odd == 1, 3, 1)

    def at(z, yy):
        return {"member": z * 4 + yy}

    pair = (jnp.where(zh % 2 == 0, zh + 1, zh - 1), 3 - zh)

    quads = [pl.ds(16 * k, 16) for k in (0, 3, 1, 2)]
    loads = [
        pltpu.make_async_copy(src, dst, load_sem.at[i])
        for i, (src, dst) in enumerate((
            *[(density.at[b], r0.at[b]) for b in quads],
            (labels_hbm, labels), (turn_hbm, turn), (value_hbm, val), (ax_hbm, axt), (ay_hbm, ayt),
            (coupling_hbm, coupling), (kernel_hbm, kern), (counts_hbm, counts),
        ))
    ]
    for c in loads[:5]:
        c.start()

    barrier = pltpu.get_barrier_semaphore()
    z_lo, core = gx // 2, gx % 2
    z_up, z_down = (zh * 4 + z_lo + 1) % 16, (zh * 4 + z_lo + 15) % 16
    beside = [{"member": (z // 4) * 4 + y, "gx": (z % 4) * 2 + core} for z in (z_up, z_down)]
    beside_y = [at(zh, (y + d) % 4) for d in (1, 3)]
    greeted = beside_y + beside
    greeted += [{"gy": (gy + d) % 4} for d in (1, 3)]

    def greet(target):
        pl.semaphore_signal(barrier, inc=1, device_id=target, device_id_type=MESH)

    has_m, has_p = gx > 0, gx < 7
    west, east = gy > 0, gy < 3
    to_m, to_p = {"gx": (gx + 7) % 8}, {"gx": (gx + 1) % 8}
    to_w, to_e = {"gy": (gy + 3) % 4}, {"gy": (gy + 1) % 4}
    pl.when(has_m)(lambda: greet(to_m))
    pl.when(has_p)(lambda: greet(to_p))
    for target in greeted:
        greet(target)

    for c in loads[5:]:
        c.start()

    def copy(i, src, dst, target):
        return pltpu.make_async_remote_copy(
            src_ref=src, dst_ref=dst, send_sem=ss.at[i], recv_sem=rs.at[i], device_id=target, device_id_type=MESH
        )

    lane = lax.broadcasted_iota(I32, (X, Y), 1)
    row = lax.broadcasted_iota(I32, (X, Y), 0)
    lane_h = lax.broadcasted_iota(I32, (32, Y), 1)

    def shift_x(r, halo, k):
        if k in (0, 3):
            return jnp.where(row == 0, halo, pltpu.roll(r, 1, 0))
        return jnp.where(row == X - 1, halo, pltpu.roll(r, X - 1, 0))

    def shift_y(r, halo, position, k):
        if k in (0, 1):
            moved_halo = pltpu.roll(halo, lax.rem(Y - position, Y), 1)
            return jnp.where(lane == 0, moved_halo, pltpu.roll(r, 1, 1))
        moved_halo = pltpu.roll(halo, Y - 1 - position, 1)
        return jnp.where(lane == Y - 1, moved_halo, pltpu.roll(r, Y - 1, 1))

    def pack_column(acc, r, position, k):
        shift = position + 1 if k in (0, 1) else position
        return jnp.where(lane == position, pltpu.roll(r, shift, 1), acc)

    for c in loads[:5]:
        c.wait()
    opened = jnp.where(labels[...] != 1, 1.0, 0.0).astype(F32)
    keep[...] = jnp.where(labels[...] == 2, 0.0, 1.0).astype(F32)
    zero_plane = jnp.zeros((X, Y), F32)

    def rows_of(ref, h0, n, x):
        return ref.reshape(H * X, Y)[pl.ds(h0 * X + x, n, stride=X), :]

    sx_p[0:16, :] = rows_of(r0, 0, 16, X - 1)
    sx_p[16:32, :] = rows_of(r0, 48, 16, X - 1)
    sx_p[32:40, :] = jnp.broadcast_to(opened[X - 1:X, :], (8, Y))
    sx_m[0:32, :] = rows_of(r0, 16, 32, 0)
    sx_m[32:40, :] = jnp.broadcast_to(opened[0:1, :], (8, Y))

    for k0, dst, shift in ((0, sy_p, 65), (2, sy_m, 64)):
        def pack(j, acc, k0=k0):
            return pack_column(acc, r0[k0 * 16 + j], j, k0)
        acc = lax.fori_loop(0, 32, pack, zero_plane, unroll=32)
        dst[...] = jnp.where(lane == 64, pltpu.roll(opened, shift, 1), acc)

    def value_row(i):
        return val.reshape(H * X, Y)[pl.ds(q * 8 + i, H, stride=X), :]

    def pack_values(rows, headings, side):
        acc = jnp.zeros((32, Y), F32)
        for i in range(8):
            part = rows[i][headings:headings + 32, :]
            shift = i + 1 if side else i
            acc = jnp.where(lane_h == i, pltpu.roll(part, shift, 1) if shift else part, acc)
        return acc

    low, high = q == 0, q == 3
    near_up = {"member": zh * 4 + jnp.where(low, y, (y + 4 - turn_sign) % 4), "gx": jnp.where(low, (gx + 7) % 8, gx)}
    near_down = {"member": zh * 4 + jnp.where(high, y, (y + turn_sign) % 4), "gx": jnp.where(high, (gx + 1) % 8, gx)}
    has_up, has_down = jnp.logical_or(q > 0, has_m), jnp.logical_or(q < 3, has_p)

    first = (
        (copy(ROW_DOWN, sx_p, hx_m, to_p), has_p, has_m),
        (copy(ROW_UP, sx_m, hx_p, to_m), has_m, has_p),
        (copy(COL_DOWN, sy_p, hy_m, to_e), east, west),
        (copy(COL_UP, sy_m, hy_p, to_w), west, east),
        (copy(VAL_DOWN, sv_p, hv_m, to_p), jnp.logical_and(high, has_p), jnp.logical_and(low, has_m)),
        (copy(VAL_UP, sv_m, hv_p, to_m), jnp.logical_and(low, has_m), jnp.logical_and(high, has_p)),
        (copy(VALCOL_DOWN, svc_p, hvc_m, to_e), east, west),
        (copy(VALCOL_UP, svc_m, hvc_p, to_w), west, east),
    )

    started, landed = [], set()

    def guarded(condition, act):
        if condition is True:
            act()
        else:
            pl.when(condition)(act)

    def launch(c, sends=True, receives=True):
        guarded(sends, c.start)
        started.append((c, sends, receives))
        return len(started) - 1

    def land(n):
        c, _, receives = started[n]
        guarded(receives, c.wait_recv)
        landed.add(n)

    sent = set()

    def settle(upto):
        for n in range(upto):
            if n not in sent:
                c, sends, _ = started[n]
                guarded(sends, c.wait_send)
                sent.add(n)

    def finish_all():
        for n in range(len(started)):
            if n not in landed:
                land(n)
        settle(len(started))

    pl.semaphore_wait(barrier, len(greeted) + has_m.astype(I32) + has_p.astype(I32))

    def pass_word(n):
        for target in beside:
            pl.semaphore_signal(word.at[n], inc=1, device_id=target, device_id_type=MESH)

    pass_word(0)
    for target in beside_y:
        pl.semaphore_signal(word_y, inc=1, device_id=target, device_id_type=MESH)
    begun = [launch(*c) for c in first[:4]]
    @pl.when(gx == 0)
    def _():
        hx_m[...] = jnp.zeros((40, Y), F32)
        hv_m[...] = jnp.zeros((32, Y), F32)
        for k in (0, 3):
            h2x[k] = jnp.zeros((16, Y), F32)

    @pl.when(gx == 7)
    def _():
        hx_p[...] = jnp.zeros((40, Y), F32)
        hv_p[...] = jnp.zeros((32, Y), F32)
        for k in (1, 2):
            h2x[k] = jnp.zeros((16, Y), F32)

    @pl.when(gy == 0)
    def _():
        for ref in (hy_m, h2y.at[0], h2y.at[1], hvc_m, hc_m):
            ref[...] = zero_plane

    @pl.when(gy == 3)
    def _():
        for ref in (hy_p, h2y.at[2], h2y.at[3], hvc_p, hc_p):
            ref[...] = zero_plane

    @pl.when(jnp.logical_not(has_up))
    def _():
        hr_m[...] = jnp.zeros((32, Y), F32)

    @pl.when(jnp.logical_not(has_down))
    def _():
        hr_p[...] = jnp.zeros((32, Y), F32)

    loads[6].wait()
    own = [value_row(i) for i in range(8)]
    svc_p[...] = pack_values(own, 32, True)
    svc_m[...] = pack_values(own, 0, False)
    sv_p[...] = own[7][16:48, :]
    sv_m[0:16, :] = own[0][0:16, :]
    sv_m[16:32, :] = own[0][48:64, :]
    begun += [launch(*c) for c in first[4:]]
    for n in (5, 7, 8, 9, 10, 11):
        loads[n].wait()
    kf[:, 0:64] = kern[...]
    kf[:, 64:128] = kern[...]
    for n in begun[:4]:
        land(n)

    open_p = jnp.where(row == X - 1, hx_p[32:33, :], pltpu.roll(opened, X - 1, 0))
    open_m = jnp.where(row == 0, hx_m[32:33, :], pltpu.roll(opened, 1, 0))
    open_e = jnp.where(lane == Y - 1, pltpu.roll(hy_p[...], 63, 1), pltpu.roll(opened, Y - 1, 1))
    open_w = jnp.where(lane == 0, pltpu.roll(hy_m[...], 64, 1), pltpu.roll(opened, 1, 1))
    weights[0] = opened * open_p
    weights[1] = opened * open_m
    weights[2] = opened * open_e
    weights[3] = opened * open_w

    def transport(k, src, dst, halo_x, x_at, halo_y, y_at, packed):
        out_x, in_x = (0, 1) if k in (0, 3) else (1, 0)
        out_y, in_y = (2, 3) if k in (0, 1) else (3, 2)
        wox, wix, woy, wiy = weights[out_x], weights[in_x], weights[out_y], weights[in_y]
        kept = keep[...]
        columns = halo_y[...]
        h0 = 16 * k

        def turns(h):
            r = src[h]
            t = turn[h].astype(F32)
            up = jnp.maximum(t, 0.0) * r
            return r, up, up - t * r

        def start_of(j):
            h = h0 + j
            r, up, down = turns(h)
            ax = axt[pl.ds(h, 1), :]
            ay = ayt[pl.ds(h, 1), :]
            hx = halo_x[pl.ds(x_at + j, 1), :]
            xn = shift_x(r, hx, k)
            yn = shift_y(r, columns, y_at + j, k)
            s = r - up - down + ax * (wix * xn - wox * r) + ay * (wiy * yn - woy * r)
            return s, up, down

        _, up_before, _ = turns((h0 + 63) % 64)
        s, up, _ = start_of(0)
        carry = (s + up_before, up, zero_plane if packed is None else packed)

        def finish(j, partial, down, acc):
            new = (partial + down) * kept
            dst[h0 + j] = new
            return acc if packed is None else pack_column(acc, new, y_at + j, k)

        def body(j, carry):
            partial, up_last, acc = carry
            s, up, down = start_of(j)
            acc = finish(j - 1, partial, down, acc)
            return s + up_last, up, acc

        partial, _, acc = lax.fori_loop(1, 16, body, carry, unroll=15)
        _, _, down = turns((h0 + 16) % 64)
        return finish(15, partial, down, acc)

    def halos(k, row_m, row_p, column_m, column_p):
        return (
            ((row_m, 0), (row_p, 0), (row_p, 16), (row_m, 16))[k]
            + ((column_m, 0), (column_m, 16), (column_p, 0), (column_p, 16))[k]
        )

    second = []
    for k in range(4):
        s2y[k] = transport(k, r0, r1, *halos(k, hx_m, hx_p, hy_m, hy_p), zero_plane)
        s2x[k] = rows_of(r1, 16 * k, 16, X - 1 if k in (0, 3) else 0)
        target = (to_p, has_p, has_m) if k in (0, 3) else (to_m, has_m, has_p)
        second.append(launch(copy(STEP_ROW + k, s2x.at[k], h2x.at[k], target[0]), *target[1:]))
        target = (to_e, east, west) if k in (0, 1) else (to_w, west, east)
        second.append(launch(copy(STEP_COL + k, s2y.at[k], h2y.at[k], target[0]), *target[1:]))

    pl.semaphore_wait(word_y, 2)
    pl.semaphore_wait(word.at[0], 2)
    pass_word(1)

    over_y = [[] for _ in range(CHUNKS)]
    for k in range(4):
        for n in second[2 * k:2 * k + 2]:
            land(n)
        transport(k, r1, r2, h2x.at[k], 0, h2y.at[k], (0, 16, 0, 16)[k], None)
        for c in range(k * CHUNKS // 4, (k + 1) * CHUNKS // 4):
            for d in (2, 1, 3):
                yy = (y + d) % 4
                qq = jnp.where(odd == 1, 3 - yy, yy)
                part = r2[pl.ds(CHUNK * c, CHUNK), pl.ds(pl.multiple_of(qq * 8, 8), 8), :]
                ysend[c, d - 1] = encode(part.reshape(ROWS, Y) * (1.0 / BOUND))
                there = copy(OVER_Y + 3 * c + d - 1, ysend.at[c, d - 1], yrecv.at[c, d - 1], at(zh, yy))
                over_y[c].append(launch(there))
    pl.semaphore_wait(word.at[1], 2)
    pass_word(2)

    def count(z, yy):
        return counts[z * 4 + yy].astype(F32)

    def plane_of(scalar):
        return jnp.full((8, Y), scalar, F32)

    def group(z):
        return count(z, 0) + count(z, 1) + count(z, 2) + count(z, 3)

    mine, across = group(zh), [group(p) for p in pair]
    everyone = group(0) + group(1) + group(2) + group(3)
    inverse_all = 1.0 / plane_of(everyone)
    inverse_mine = (1.0 / BOUND) / plane_of(mine)

    def scaled(part, factor):
        return (part.reshape(CHUNK, 8, Y) * factor).reshape(ROWS, Y)

    for n in begun[4:]:
        land(n)

    @pl.when(low)
    def _():
        up_row[...] = hv_m[...]

    @pl.when(q > 0)
    def _():
        up_row[...] = val.reshape(H * X, Y)[pl.ds(16 * X + q * 8 - 1, 32, stride=X), :]

    @pl.when(high)
    def _():
        down_row[...] = hv_p[...]

    @pl.when(q < 3)
    def _():
        down_row[0:16, :] = val.reshape(H * X, Y)[pl.ds(q * 8 + 8, 16, stride=X), :]
        down_row[16:32, :] = val.reshape(H * X, Y)[pl.ds(48 * X + q * 8 + 8, 16, stride=X), :]

    wide_rows = pl.ds(pl.multiple_of(q * 8, 8), 8)
    w_rows = [weights[i, wide_rows, :] for i in range(4)]
    keep_rows = keep[wide_rows, :]
    kf_high, kf_low = split_left(kf[...])
    lane_c = lax.broadcasted_iota(I32, (64, 2 * Y), 1)
    kb = jnp.concatenate([kf_high, kf_low], axis=1)
    cf[:, 0:64] = coupling[...]
    cf[:, 64:128] = coupling[...]
    cf_high, cf_low = split_left(cf[...])
    cb = jnp.concatenate([cf_high, cf_low], axis=1)

    lane_of = lax.broadcasted_iota(I32, (32, Y), 1)

    def around(rows, before, after, first_column, last_column, i):
        v = rows[i]
        prior = rows[i - 1][16:48, :] if i > 0 else before
        if i < 7:
            later = (rows[i + 1][0:16, :], rows[i + 1][48:64, :])
        else:
            later = (after[0:16, :], after[16:32, :])
        north, south = pltpu.roll(v[0:32, :], Y - 1, 1), pltpu.roll(v[32:64, :], 1, 1)
        if last_column is not None:
            north = jnp.where(lane_of == Y - 1, pltpu.roll(last_column, Y - 1 - i, 1), north)
            south = jnp.where(lane_of == 0, pltpu.roll(first_column, Y - i, 1) if i else first_column, south)
        return v, prior, later, north, south, [w[i:i + 1, :] for w in w_rows]

    def reply(jobs):
        lowest_of, parts = [], []
        for v, prior, later, north, south, w in jobs:
            moves = []
            for k in range(4):
                part = slice(16 * k, 16 * k + 16)
                vk = v[part, :]
                xn = (later[0], prior[0:16, :], prior[16:32, :], later[1])[k]
                yn = (north[0:16, :], north[16:32, :], south[0:16, :], south[16:32, :])[k]
                wx = w[0 if k in (0, 3) else 1]
                wy = w[2 if k in (0, 1) else 3]
                moves.append(vk + axt[part, :] * (wx * (xn - vk)) + ayt[part, :] * (wy * (yn - vk)))
            moves = jnp.concatenate(moves, axis=0)
            lowest = jnp.min(moves, axis=0, keepdims=True)
            lowest_of.append(lowest)
            parts.append(jnp.exp((lowest - moves) * 10.0))
        summed = jnp.dot(cb, widen(jnp.concatenate(parts, axis=1)), preferred_element_type=F32)
        logs = jnp.log(summed) * 0.1
        return [lowest_of[n] - logs[:, n * Y:(n + 1) * Y] for n in range(len(jobs))]

    row_8 = lax.broadcasted_iota(I32, (8, Y), 0)
    lane_8 = lax.broadcasted_iota(I32, (8, Y), 1)

    def sides_of(w):
        first = jnp.where(lane_8 == row_8, w[:, 0:1], 0.0)
        last = jnp.where(lane_8 == row_8 + 8, w[:, Y - 1:Y], 0.0)
        return jnp.sum(first + last, axis=0, keepdims=True)

    w_sides = [sides_of(w) for w in w_rows]
    keep_sides = sides_of(keep_rows)

    def side_by_side(rows, first, last, part):
        acc = jnp.zeros((part.stop - part.start, Y), F32)
        lanes = lax.broadcasted_iota(I32, acc.shape, 1)
        for i in range(8):
            if first is not None:
                acc = jnp.where(lanes == i, pltpu.roll(rows[i][part, :], (i - first) % Y, 1), acc)
            if last is not None:
                acc = jnp.where(lanes == 8 + i, pltpu.roll(rows[i][part, :], (8 + i - last) % Y, 1), acc)
        return acc

    from_start = reply([around(own, up_row[...], down_row[...], hvc_m[...], hvc_p[...], i) for i in range(8)])
    for i in range(8):
        base[i] = from_start[i]

    pl.semaphore_wait(word.at[2], 2)
    over_z = [[None, None] for _ in range(CHUNKS)]
    for c in range(CHUNKS):
        block = pl.ds(CHUNK * c, CHUNK)
        part = r2[block, pl.ds(pl.multiple_of(q * 8, 8), 8), :].reshape(ROWS, Y) * count(zh, y)
        for n, d in zip(over_y[c], (2, 1, 3)):
            land(n)
            part = part + decode(yrecv[c, d - 1]) * count(zh, (y + 4 - d) % 4)
        zsend[c, 0] = encode(scaled(part, inverse_mine))
        over_z[c][0] = launch(copy(OVER_Z + 2 * c, zsend.at[c, 0], zrecv.at[c, 0], at(pair[c % 2], y)))

    lower = [jnp.full((8, Y), zh, I32) < jnp.full((8, Y), p, I32) for p in pair]

    def merge(c, stage, partner, weight_own, weight_other):
        a = decode(zsend[c, stage]).reshape(CHUNK, 8, Y) * weight_own
        b = decode(zrecv[c, stage]).reshape(CHUNK, 8, Y) * weight_other
        is_low = lower[partner]
        return jnp.where(is_low, a, b) + jnp.where(is_low, b, a)

    factors = [(1.0 / BOUND) / plane_of(mine + across[p]) for p in range(2)]
    for c in range(CHUNKS):
        p = c % 2
        land(over_z[c][0])
        both = merge(c, 0, p, mine, across[p])
        zsend[c, 1] = encode((both * factors[p]).reshape(ROWS, Y))
        over_z[c][1] = launch(copy(OVER_Z + 2 * c + 1, zsend.at[c, 1], zrecv.at[c, 1], at(pair[1 - p], y)))
    for c in range(CHUNKS):
        p = c % 2
        land(over_z[c][1])
        here = mine + across[p]
        mixed = merge(c, 1, 1 - p, here, everyone - here) * inverse_all
        total[pl.ds(ROWS * c, ROWS), :] = mixed.reshape(ROWS, Y)

    mixed_rows = jnp.concatenate([total[pl.ds(i, H, stride=8), :] for i in range(8)], axis=1)
    running = 0.5 + 0.5 * jnp.dot(kb, widen(mixed_rows), preferred_element_type=F32)
    cost = [running[:, i * Y:(i + 1) * Y] for i in range(8)]
    once = [(cost[i] + base[i]) * keep_rows[i:i + 1, :] for i in range(8)]

    sr_p[...] = once[7][16:48, :]
    sr_m[0:16, :] = once[0][0:16, :]
    sr_m[16:32, :] = once[0][48:64, :]
    before_edges = len(started)
    edges = [
        launch(copy(REPLY, sr_p, hr_m, near_down), has_down, has_up),
        launch(copy(REPLY + 1, sr_m, hr_p, near_up), has_up, has_down),
    ]
    sc_p[...] = pack_values(once, 32, True)
    edges.append(launch(copy(REPLY + 2, sc_p, hc_m, to_e), east, west))
    sc_m[...] = pack_values(once, 0, False)
    edges.append(launch(copy(REPLY + 3, sc_m, hc_p, to_w), west, east))

    def code_of(v, eighths):
        inverse = (32767.0 * 8.0) / eighths.astype(F32)
        return ((v * inverse + 32768.5).astype(I32) - 32768).astype(I16)

    def eighths_of(v):
        return (jnp.max(jnp.abs(v), axis=0, keepdims=True) * 8.0).astype(I32) + 1

    def send_piece(piece, rows, tile):
        for n in range(SPAN):
            gsend[piece, pl.ds(H * n, H), :] = rows[n]
        gsend[piece, pl.ds(MARK, 16), :] = tile
        out = []
        for d in (2, 1, 3):
            there = copy(GATHER + 3 * piece + d - 1, gsend.at[piece], grecv.at[piece, d - 1], at(zh, (y + d) % 4))
            out.append((launch(there), piece, d))
        return out

    def closed(i, t):
        return (cost[i] + t) * keep_rows[i:i + 1, :]

    gathers = []
    for piece in range(PIECES - 1):
        indices = (2 * piece + 1, 2 * piece + 2)
        twice = [closed(i, t) for i, t in zip(indices, reply([around(once, None, None, None, None, i) for i in indices]))]
        eighths = eighths_of(jnp.concatenate(twice, axis=0))
        tile = jnp.broadcast_to(eighths, (16, Y)).astype(I16)
        gathers += send_piece(piece, [code_of(v, eighths) for v in twice], tile)
    settle(before_edges)
    whole = slice(0, H)
    sides = side_by_side(once, 0, Y - 1, whole)
    cost_sides = side_by_side(cost, 0, Y - 1, whole)
    inner_first = side_by_side(once, 1, None, slice(0, 32))
    inner_last = side_by_side(once, None, Y - 2, slice(32, H))
    after_sides, before_sides = pltpu.roll(sides, Y - 1, 1), pltpu.roll(sides, 1, 1)
    for n in edges:
        land(n)
    last_three = reply((
        around(once, hr_m[...], hr_p[...], hc_m[...], hc_p[...], 0),
        around(once, hr_m[...], hr_p[...], hc_m[...], hc_p[...], 7),
        (
            sides, before_sides[16:48, :], (after_sides[0:16, :], after_sides[48:64, :]),
            jnp.where(lane_of < 8, inner_first, pltpu.roll(hc_p[...], 8, 1)),
            jnp.where(lane_of < 8, hc_m[...], inner_last), w_sides,
        ),
    ))
    ends = (closed(0, last_three[0]), closed(7, last_three[1]))
    columns = (cost_sides + last_three[2]) * keep_sides
    patch = columns[0:8, :]
    for n in range(1, 8):
        here = jnp.logical_and(lane_8 >= 16 * n, lane_8 < 16 * n + 16)
        patch = jnp.where(here, pltpu.roll(columns[8 * n:8 * n + 8, :], 16 * n, 1), patch)
    eighths = eighths_of(jnp.concatenate(ends, axis=0))
    eighths_patch = eighths_of(patch)
    scales = jnp.where(row_8 < 4, eighths, eighths_patch)
    inverse = (32767.0 * 8.0) / eighths_patch.astype(F32)
    patch_code = (patch * inverse + 32768.5).astype(I32) - 32768
    tile = jnp.concatenate([scales, patch_code], axis=0).astype(I16)
    gathers += send_piece(PIECES - 1, [code_of(v, eighths) for v in ends], tile)

    lane_w = lax.broadcasted_iota(I32, (H, Y), 1)
    out_rows = out.reshape(H * X, Y)

    def unpack(codes, qq, piece):
        scale = codes[MARK:MARK + 1, :].astype(F32) * (0.125 / 32767.0)
        indices = (2 * piece + 1, 2 * piece + 2) if piece < PIECES - 1 else (0, 7)
        for n, i in enumerate(indices):
            out_rows[pl.ds(qq * 8 + i, H, stride=X), :] = codes[H * n:H * n + H, :].astype(F32) * scale
        if piece < PIECES - 1:
            return
        scale = codes[MARK + 4:MARK + 5, :].astype(F32) * (0.125 / 32767.0)
        flat = codes[MARK + 8:MARK + 16, :].astype(F32) * scale
        wide = jnp.concatenate([pltpu.roll(flat, Y - 16 * n, 1) if n else flat for n in range(8)], axis=0)
        for i in range(1, 7):
            at_row = pl.ds(qq * 8 + i, H, stride=X)
            v = jnp.where(lane_w == 0, pltpu.roll(wide, Y - i, 1), out_rows[at_row, :])
            out_rows[at_row, :] = jnp.where(lane_w == Y - 1, pltpu.roll(wide, Y - 9 - i, 1), v)

    for piece in range(PIECES):
        unpack(gsend[piece].astype(I32), q, piece)
    settle(len(started) - 3)
    for n, piece, d in sorted(gathers, key=lambda g: (g[1], g[2] == 2)):
        land(n)
        yy = (y + 4 - d) % 4
        unpack(grecv[piece, d - 1].astype(I32), jnp.where(odd == 1, 3 - yy, yy), piece)
    finish_all()


def write_out(moved, values, moved_out, values_out, sems):
    copies = [
        pltpu.make_async_copy(src, dst, sems.at[i])
        for i, (src, dst) in enumerate(((moved, moved_out), (values, values_out)))
    ]
    for c in copies:
        c.start()
    for c in copies:
        c.wait()


def shards(density, turn_rate, value_init, labels, counts, kernel_matrix):
    along_x, along_y, coupling = tables()
    vmem = lambda *shape: pltpu.VMEM(shape, F32)
    in_hbm = pl.BlockSpec(memory_space=pltpu.HBM)
    scratch = [
        vmem(H, X, Y), pltpu.VMEM((H, X, Y), BF16), vmem(H, X, Y), pltpu.VMEM((X, Y), I32), vmem(H, Y), vmem(H, Y),
        vmem(H, H), vmem(H, H),
        vmem(40, Y), vmem(40, Y), *[vmem(32, Y) for _ in range(6)],
        vmem(40, Y), vmem(40, Y), *[vmem(32, Y) for _ in range(6)],
        vmem(H, X, Y), vmem(4, 16, Y), vmem(4, X, Y), vmem(4, 16, Y), vmem(4, X, Y), vmem(4, X, Y),
        vmem(X, Y),
        pltpu.VMEM((CHUNKS, 3, ROWS, Y), I16), pltpu.VMEM((CHUNKS, 3, ROWS, Y), I16),
        pltpu.VMEM((CHUNKS, 2, ROWS, Y), I16), pltpu.VMEM((CHUNKS, 2, ROWS, Y), I16), vmem(512, Y), vmem(8, H, Y),
        vmem(32, Y), vmem(32, Y), vmem(8, Y), vmem(H, 128), vmem(H, 128),
        *[vmem(32, Y) for _ in range(8)],
        pltpu.VMEM((PIECES, MARK + 16, Y), I16), pltpu.VMEM((PIECES, 3, MARK + 16, Y), I16),
        pltpu.SMEM((16,), I32), pltpu.SemaphoreType.REGULAR((3,)), pltpu.SemaphoreType.REGULAR, pltpu.SemaphoreType.DMA((12,)),
        pltpu.SemaphoreType.DMA((COPIES,)), pltpu.SemaphoreType.DMA((COPIES,)),
    ]
    held = pltpu.VMEM((H, X, Y), F32)
    in_vmem = pl.BlockSpec(memory_space=pltpu.VMEM)
    operands = (
        counts, density[0], turn_rate[0], value_init, labels,
        jnp.asarray(along_x), jnp.asarray(along_y), jnp.asarray(coupling), kernel_matrix,
    )
    moved, values = pl.pallas_call(
        kernel,
        out_shape=(held, held),
        in_specs=[in_hbm] * 9,
        out_specs=(in_vmem, in_vmem),
        scratch_shapes=scratch,
        compiler_params=pltpu.CompilerParams(
            collective_id=1, has_side_effects=True, vmem_limit_bytes=40 * 1024 * 1024
        ),
        name="play",
    )(*[pltpu.with_memory_space_constraint(a, pltpu.HBM) for a in operands])
    whole = jax.ShapeDtypeStruct((H, X, Y), F32)
    moved, values = pl.pallas_call(
        write_out,
        out_shape=(whole, whole),
        in_specs=[in_vmem, in_vmem],
        out_specs=(in_hbm, in_hbm),
        scratch_shapes=[pltpu.SemaphoreType.DMA((2,))],
        compiler_params=pltpu.CompilerParams(vmem_limit_bytes=8 * 1024 * 1024),
        name="write",
    )(moved, values)
    return moved[None], values


def solution(mesh):
    placed = (
        P("member", None, "gx", "gy"),
        P("member", None, "gx", "gy"),
        P(None, "gx", "gy"),
        P("gx", "gy"),
        P(),
        P(),
    )
    return jax.shard_map(
        shards,
        mesh=mesh,
        in_specs=placed,
        out_specs=(P("member", None, "gx", "gy"), P(None, "gx", "gy")),
        check_vma=False,
    )
```
